128 devices in a mesh: cells: 16 (over y_hi, z, core), grow: 4 (over x), gcol: 2 (over y_lo).
Axes of the slice: x: 4, y: 4 (y_hi: 2, y_lo: 2; y = y_hi * 2 + y_lo), z: 4, core: 2. Of those that a mesh axis runs over, the one named last changes fastest.
Arguments:
- counts: int32 [18432, 4, 2, 1024], P('cells', 'grow', 'gcol'), may hold values from 0 to 2689, as said below
- gene_mean: float32 [4, 2, 1024], P('grow', 'gcol'), may hold values from 0.2 to 1.2
- gene_scale: float32 [4, 2, 1024], P('grow', 'gcol'), may hold values from 0.4 to 2
Outputs:
- coexpression: float32 [4, 2048, 2, 4, 1024], P('grow', 'cells', 'gcol')
The draws below stay inside these ranges and needn't reach their ends.
Inputs may be any that keep to these rules, and one draw needn't show every extreme that they name: `counts`: every cell has at least one count.
All inputs are finite; a program needn't handle non-finite values.
Results may differ from the reference program's by a relative error of at most 0.0008.
Values may be sent and summed in bfloat16 or wider, within the bound.
No kernel may reach another device: no remote copies, remote signals or barrier semaphores. Data moves between devices by JAX's collectives and lax.ppermute only.
A program may use at most 384 MiB of HBM per device.

```python
import math
import jax
import jax.numpy as jnp
from jax import lax

GENES = 8192
CELLS = 18432
SPAN = 1024
N_GROW = 4
N_GCOL = 2


def draw_counts(key, part):
    key = jax.random.fold_in(key, 11)
    key_cell, key_gene, key_value, key_pick, key_load, key_first, key_second = jax.random.split(key, 7)
    programs = max(GENES // 8, 4)
    cell_shift = jax.random.randint(key_cell, (CELLS,), 0, 5)
    cell_shift = cell_shift.at[0].set(4)
    gene_shift = jax.random.randint(key_gene, (GENES,), 0, 4)
    gene_shift = gene_shift.at[GENES - 1].set(3)
    genes = jnp.arange(GENES, dtype=jnp.int32)
    ramp = 1 + 3 * genes // GENES
    first = jax.random.randint(key_first, (GENES,), 0, programs)
    second = jax.random.randint(key_second, (GENES,), 0, programs)
    loading = jax.random.randint(key_load, (CELLS, programs), 0, 4)
    loading = loading.at[0, first[GENES - 1]].set(3)
    loading = loading.at[0, second[GENES - 1]].set(3)
    activity = 1 + jnp.take(loading, first, axis=1) + jnp.take(loading, second, axis=1)
    cell_level = jnp.left_shift(jnp.int32(1), cell_shift)
    gene_level = jnp.left_shift(jnp.int32(1), gene_shift) * ramp
    upper = cell_level[:, None] * gene_level[None, :] * activity
    values = jax.random.randint(key_value, (CELLS, GENES), 0, upper + 1)
    values = values.at[0, GENES - 1].set(upper[0, GENES - 1])
    picked = jax.random.randint(key_pick, (CELLS,), 0, GENES)
    picked = picked.at[0].set(GENES - 1)
    values = values + (genes[None, :] == picked[:, None]).astype(jnp.int32)
    return values.reshape(CELLS, N_GROW, N_GCOL, GENES // (N_GROW * N_GCOL)).astype(jnp.int32)


def levels(rng, shape, cuts, least, top_value):
    factor_of, own = 1.0, jax.random.fold_in(rng, 6)
    for dim, blocks in cuts:
        draws = jnp.exp(jax.random.uniform(jax.random.fold_in(own, dim), (blocks,), jnp.float32, least / len(cuts), top_value / len(cuts)))
        factor_of = factor_of * jnp.repeat(draws, shape[dim] // blocks).reshape([-1 if axis == dim else 1 for axis in range(len(shape))])
    return factor_of


def setup_inputs(seed: int = 0) -> dict:
    seeds = jax.random.split(jax.random.key(seed), 4)
    counts = draw_counts(jax.random.fold_in(seeds[3], 71), 0)
    gene_mean = jnp.clip(0.2 + 1 * jax.random.uniform(seeds[1], (N_GROW, N_GCOL, SPAN), jnp.float32) ** levels(seeds[1], (N_GROW, N_GCOL, SPAN), ((0, 4), (1, 2)), -0.2, 0.2), 0.2, 1.2)
    gene_scale = jnp.clip(jnp.exp(math.log(2.0) - 1.609438 * jax.random.uniform(seeds[2], (N_GROW, N_GCOL, SPAN), jnp.float32) ** levels(seeds[2], (N_GROW, N_GCOL, SPAN), ((0, 4), (1, 2)), -0.2, 0.2)), 0.4, 2.0)
    return {"counts": counts, "gene_mean": gene_mean, "gene_scale": gene_scale}


def reference(counts, gene_mean, gene_scale):
    flat = counts.reshape(CELLS, GENES).astype(jnp.float32)
    totals = jnp.sum(flat, axis=1)
    lognorm = jnp.log1p(flat * GENES / totals[:, None])
    standard = ((lognorm - gene_mean.reshape(GENES)[None, :]) / gene_scale.reshape(GENES)[None, :]).astype(jnp.bfloat16)
    values = standard.astype(jnp.float32)
    gram = lax.dot_general(values, values, (((0,), (0,)), ((), ())), precision=lax.Precision.HIGHEST, preferred_element_type=jnp.float32)
    gram = gram / CELLS
    gram = gram.reshape(GENES, N_GROW, N_GCOL, SPAN).transpose(0, 2, 1, 3)
    return gram.reshape(N_GROW, GENES // N_GROW, N_GCOL, N_GROW, SPAN)
```

```python
import jax
import jax.numpy as jnp
import numpy as np
from jax import lax
from jax.experimental import pallas as pl
from jax.experimental.pallas import tpu as pltpu
from jax.sharding import PartitionSpec as P

GENES = 8192
CELLS = 18432
AXES = ("cells", "grow", "gcol")
SIZES = (2, 4, 2, 4, 2)
ROWS = 1152
DEPTH = 2 * ROWS
HALF = 512
ORDER = (0, 3, 2, 1)

ALPHA = 2.0**17 / 9.0e6
BETA = 32700.0 / float(np.log1p(2.0**17))
VMEM = 60 * 1024 * 1024


def moves(target):
    pairs = []
    for i, at in enumerate(np.ndindex(*SIZES)):
        to = tuple(v % s for v, s in zip(target(*at), SIZES))
        pairs.append((i, int(np.ravel_multi_index(to, SIZES))))
    return pairs


TO_CORE = moves(lambda h, z, c, x, b: (h, z, 1 - c, x, b))
TO_YLO = moves(lambda h, z, c, x, b: (h, z, c, x, 1 - b))
TO_YHI = moves(lambda h, z, c, x, b: (1 - h, z, c, x, b))
TO_YHI_CORE = moves(lambda h, z, c, x, b: (1 - h, z, 1 - c, x, b))
TO_X1 = moves(lambda h, z, c, x, b: (h, z, c, x ^ 1, b))
TO_X3 = moves(lambda h, z, c, x, b: (h, z, c, x ^ 3, b))
TO_Z1 = moves(lambda h, z, c, x, b: (h, z ^ 1, c, x, b))
TO_Z3 = moves(lambda h, z, c, x, b: (h, z ^ 3, c, x, b))
TO_SAME = moves(lambda h, z, c, x, b: (h, z, c, x - 1 + 2 * c, b))
TO_CROSS = moves(lambda h, z, c, x, b: (h, z, 1 - c, x + 1 - 2 * c, b))


def send(value, pairs):
    return lax.ppermute(value, AXES, pairs)


def encode(total):
    size = jnp.log(1.0 + ALPHA * jnp.abs(total)) * BETA + 0.5
    code = size.astype(jnp.int32)
    return jnp.where(total < 0, -code, code).astype(jnp.int16)


def decode(code):
    code = code.astype(jnp.int32).astype(jnp.float32)
    size = (jnp.exp(jnp.abs(code) * (1.0 / BETA)) - 1.0) * (1.0 / ALPHA)
    return jnp.where(code < 0, -size, size)


def params(flops=0, byte=0):
    return dict(
        compiler_params=pltpu.CompilerParams(vmem_limit_bytes=VMEM),
        cost_estimate=pl.CostEstimate(flops=flops, bytes_accessed=byte, transcendentals=0),
    )


def of(shape, dtype):
    return jax.ShapeDtypeStruct(shape, dtype)


def narrow(counts, core):
    steps = 8
    tile = ROWS // steps

    def body(core_ref, counts_ref, whole_ref, mine_ref, other_ref):
        whole_ref[...] = counts_ref[...].astype(jnp.int16)
        mine = core_ref[0]
        mine_ref[...] = counts_ref[:, pl.ds(pl.multiple_of(mine * HALF, HALF), HALF)].astype(jnp.int16)
        other_ref[...] = counts_ref[:, pl.ds(pl.multiple_of((1 - mine) * HALF, HALF), HALF)].astype(jnp.int16)

    return pl.pallas_call(
        body,
        out_shape=(of((ROWS, 1024), jnp.int16), of((ROWS, HALF), jnp.int16), of((ROWS, HALF), jnp.int16)),
        grid_spec=pltpu.PrefetchScalarGridSpec(
            num_scalar_prefetch=1,
            grid=(steps,),
            in_specs=[pl.BlockSpec((tile, 1024), lambda i, s: (i, 0))],
            out_specs=[
                pl.BlockSpec((tile, 1024), lambda i, s: (i, 0)),
                pl.BlockSpec((tile, HALF), lambda i, s: (i, 0)),
                pl.BlockSpec((tile, HALF), lambda i, s: (i, 0)),
            ],
        ),
        **params(byte=10 << 20),
    )(core, counts)


def standardized(count, factor, gene):
    value = count.astype(jnp.int32).astype(jnp.float32)
    return (jnp.log(1.0 + value * factor) * gene[0:1, :] - gene[1:2, :]).astype(jnp.bfloat16)


def row_groups(mine, sibling, factors, gene, z):
    order = jnp.array(ORDER, jnp.int32)
    lanes = jnp.concatenate([(order ^ z) * 2, (order ^ z) * 2 + 1])

    def body(lane_ref, mine_ref, sibling_ref, f_ref, g_ref, out_ref):
        gene_of = g_ref[...]
        out_ref[0, :, 0:ROWS] = standardized(mine_ref[...], f_ref[0:ROWS, :], gene_of).T
        out_ref[0, :, ROWS:DEPTH] = standardized(sibling_ref[...], f_ref[ROWS:DEPTH, :], gene_of).T

    return pl.pallas_call(
        body,
        out_shape=of((2, HALF, DEPTH), jnp.bfloat16),
        grid_spec=pltpu.PrefetchScalarGridSpec(
            num_scalar_prefetch=1,
            grid=(8,),
            in_specs=[
                pl.BlockSpec((ROWS, 128), lambda i, s: (0, s[i])),
                pl.BlockSpec((ROWS, 128), lambda i, s: (0, s[i])),
                pl.BlockSpec((DEPTH, 1), lambda i, s: (0, 0)),
                pl.BlockSpec((2, 128), lambda i, s: (0, s[i])),
            ],
            out_specs=pl.BlockSpec((1, 128, DEPTH), lambda i, s: (i // 4, i % 4, 0)),
        ),
        **params(byte=10 << 20),
    )(lanes, mine, sibling, factors, gene)


def column_chunks(pieces, factors):
    n = len(pieces)
    tiles = 4
    offsets = jnp.stack([jnp.asarray(p[3], jnp.int32) for p in pieces])

    def body(off_ref, *refs):
        out_ref = refs[-1]
        f_ref = refs[3 * n]
        i = pl.program_id(0)
        for k in range(n):

            @pl.when(i // tiles == k)
            def _():
                mine_ref, sibling_ref, g_ref = refs[3 * k : 3 * k + 3]
                gene_of = g_ref[...]
                out_ref[0, 0:ROWS, :] = standardized(mine_ref[...], f_ref[0:ROWS, :], gene_of)
                out_ref[0, ROWS:DEPTH, :] = standardized(sibling_ref[...], f_ref[ROWS:DEPTH, :], gene_of)

    def at(k):
        return lambda i, s: (0, s[k] * tiles + jnp.clip(i - k * tiles, 0, tiles - 1))

    in_specs, operands = [], []
    for k, (mine, sibling, gene, _) in enumerate(pieces):
        in_specs += [
            pl.BlockSpec((ROWS, 128), at(k)),
            pl.BlockSpec((ROWS, 128), at(k)),
            pl.BlockSpec((2, 128), at(k)),
        ]
        operands += [mine, sibling, gene]
    in_specs.append(pl.BlockSpec((DEPTH, 1), lambda i, s: (0, 0)))
    return pl.pallas_call(
        body,
        out_shape=of((n, DEPTH, HALF), jnp.bfloat16),
        grid_spec=pltpu.PrefetchScalarGridSpec(
            num_scalar_prefetch=1,
            grid=(n * tiles,),
            in_specs=in_specs,
            out_specs=pl.BlockSpec((1, DEPTH, 128), lambda i, s: (i // tiles, 0, i % tiles)),
        ),
        **params(byte=n * (5 << 20)),
    )(offsets, *operands, factors)


def products(steps, rows, cols):
    n = len(steps)
    combos = sorted({(r, c) for r, _, c, _ in steps})
    which = jnp.array([combos.index((r, c)) for r, _, c, _ in steps], jnp.int32)

    def last(array, place):
        table, now = [], next(s[place + 1] for s in steps if s[place] == array)
        for s in steps:
            now = s[place + 1] if s[place] == array else now
            table.append(now)
        return jnp.array(table, jnp.int32)

    tables = [last(r, 0) for r in range(len(rows))] + [last(c, 2) for c in range(len(cols))]

    def body(which_ref, *refs):
        refs = refs[len(tables) :]
        row_refs, col_refs = refs[: len(rows)], refs[len(rows) : len(rows) + len(cols)]
        send_a, send_b, keep_a, keep_b = refs[len(rows) + len(cols) :]
        for k, (r, c) in enumerate(combos):

            @pl.when(which_ref[pl.program_id(0)] == k)
            def _():
                left = row_refs[r][0]
                a = jnp.dot(left, col_refs[c][0, :, 0:256], preferred_element_type=jnp.float32)
                keep_a[0] = a[0:256].reshape(2, 128, 256)
                send_a[0] = encode(a[256:512]).reshape(2, 128, 256)
                b = jnp.dot(left, col_refs[c][0, :, 256:512], preferred_element_type=jnp.float32)
                keep_b[0, 0] = b[0:128]
                keep_b[0, 1] = b[384:512]
                send_b[0] = encode(b[128:384]).reshape(2, 128, 256)

    def row_map(k):
        return lambda i, which, *t: (t[k][i], 0, 0)

    in_specs = [pl.BlockSpec((1, HALF, DEPTH), row_map(k)) for k in range(len(rows))]
    in_specs += [pl.BlockSpec((1, DEPTH, HALF), row_map(len(rows) + k)) for k in range(len(cols))]
    out = pl.BlockSpec((1, 2, 128, 256), lambda i, *t: (i, 0, 0, 0))
    return pl.pallas_call(
        body,
        out_shape=(
            of((n, 2, 128, 256), jnp.int16),
            of((n, 2, 128, 256), jnp.int16),
            of((n, 2, 128, 256), jnp.float32),
            of((n, 2, 128, 256), jnp.float32),
        ),
        grid_spec=pltpu.PrefetchScalarGridSpec(
            num_scalar_prefetch=1 + len(tables), grid=(n,), in_specs=in_specs, out_specs=[out] * 4
        ),
        **params(flops=n * 2 * HALF * HALF * DEPTH, byte=n * (4 << 20)),
    )(which, *tables, *rows, *cols)


def second(keep_a, keep_b, got_a, got_b):
    n = keep_a.shape[0]

    def body(ka, kb, ga, gb, sa2, sb2, ka2, kb2):
        ka2[...] = ka[:, 0] + decode(ga[:, 1])
        sa2[...] = encode(ka[:, 1] + decode(ga[:, 0]))
        kb2[...] = kb[:, 0] + decode(gb[:, 0])
        sb2[...] = encode(kb[:, 1] + decode(gb[:, 1]))

    four = pl.BlockSpec((1, 2, 128, 256), lambda i: (i, 0, 0, 0))
    three = pl.BlockSpec((1, 128, 256), lambda i: (i, 0, 0))
    return pl.pallas_call(
        body,
        grid=(n,),
        out_shape=(
            of((n, 128, 256), jnp.int16),
            of((n, 128, 256), jnp.int16),
            of((n, 128, 256), jnp.float32),
            of((n, 128, 256), jnp.float32),
        ),
        in_specs=[four] * 4,
        out_specs=[three] * 4,
        **params(byte=n * (1 << 20)),
    )(keep_a, keep_b, got_a, got_b)


def summed_z(parts, groups, tables):
    chunks, rounds = len(tables), len(parts)
    used = np.array([[t[0] for t in row] for row in tables], np.int32)
    index = []
    for r in range(rounds):
        index.append(np.array([[t[1] if t[0] == r else 0 for t in row] for row in tables], np.int32))
    pick = jnp.stack([jnp.asarray(t)[:, groups].reshape(-1) for t in [used, *index]])

    def body(pick_ref, *refs):
        keep, to_c, to_y, to_yc = refs[4 * rounds :]
        i = pl.program_id(0)
        for r in range(rounds):

            @pl.when(pick_ref[0, i] == r)
            def _():
                ka, kb, ga, gb = refs[4 * r : 4 * r + 4]
                a, b = ka[0] + decode(ga[0]), kb[0] + decode(gb[0])

                @pl.when(i % 4 == 0)
                def _():
                    keep[0, :, 0:256] = a
                    keep[0, :, 256:512] = b

                for d, ref in ((1, to_c), (2, to_y), (3, to_yc)):

                    @pl.when(i % 4 == d)
                    def _():
                        ref[0, :, 0:256] = encode(a)
                        ref[0, :, 256:512] = encode(b)

    def at(r):
        return lambda i, s: (s[1 + r, i], 0, 0)

    in_specs = [pl.BlockSpec((1, 128, 256), at(r)) for r in range(rounds) for _ in range(4)]
    return pl.pallas_call(
        body,
        out_shape=(of((chunks, 128, HALF), jnp.float32),) + (of((chunks, 128, HALF), jnp.int16),) * 3,
        grid_spec=pltpu.PrefetchScalarGridSpec(
            num_scalar_prefetch=1,
            grid=(chunks * 4,),
            in_specs=in_specs,
            out_specs=[pl.BlockSpec((1, 128, HALF), lambda i, s: (i // 4, 0, 0))] * 4,
        ),
        **params(byte=chunks * (2 << 20)),
    )(pick, *[a for part in parts for a in part])


def finish(keep, got_c, got_y, got_yc, places, out=None):
    n = keep.shape[0]

    def body(place_ref, keep_ref, y_ref, c_ref, yc_ref, *rest):
        out_ref = rest[-1]
        i = pl.program_id(0)

        @pl.when(i < n)
        def _():
            out_ref[...] = (keep_ref[0] + decode(y_ref[0])) * (1.0 / CELLS)

        @pl.when(i >= n)
        def _():
            out_ref[...] = (decode(c_ref[0]) + decode(yc_ref[0])) * (1.0 / CELLS)

    mine = pl.BlockSpec((1, 128, HALF), lambda i, s: (jnp.minimum(i, n - 1), 0, 0))
    other = pl.BlockSpec((1, 128, HALF), lambda i, s: (jnp.maximum(i - n, 0), 0, 0))
    in_specs, operands, alias = [mine, mine, other, other], [keep, got_y, got_c, got_yc], {}
    if out is not None:
        in_specs.append(pl.BlockSpec(memory_space=pl.ANY))
        operands.append(out)
        alias = {5: 0}
    return pl.pallas_call(
        body,
        out_shape=of((128, 4096), jnp.float32),
        grid_spec=pltpu.PrefetchScalarGridSpec(
            num_scalar_prefetch=1,
            grid=(2 * n,),
            in_specs=in_specs,
            out_specs=pl.BlockSpec((128, HALF), lambda i, s: (0, s[i])),
        ),
        input_output_aliases=alias,
        **params(byte=n * (1 << 20)),
    )(places, *operands)


def per_device(counts, gene_mean, gene_scale):
    cells, x, b = lax.axis_index("cells"), lax.axis_index("grow"), lax.axis_index("gcol")
    high, z, core = cells // 8, (cells // 2) % 4, cells % 2
    counts = counts.reshape(ROWS, 1024)

    whole, first, other = narrow(counts, core.reshape(1))
    n0_mine, n0_sib = send(first, TO_SAME), send(other, TO_CROSS)
    y_mine = send(whole, TO_YLO)
    n1_mine, n1_sib = send(other, TO_SAME), send(first, TO_CROSS)
    whole_sib = send(whole, TO_CORE)

    inverse = 1.0 / gene_scale.reshape(1024)
    own = jnp.concatenate([inverse, gene_mean.reshape(1024) * inverse])
    total = jnp.sum(counts, axis=1).astype(jnp.float32)
    got = send(jnp.concatenate([total, own]), TO_YLO)
    total, gene_y = total + got[:ROWS], got[ROWS:]
    got = send(jnp.concatenate([total, own]), TO_X1)
    total, gene_1 = total + got[:ROWS], got[ROWS:]
    got = send(jnp.concatenate([total, own, gene_1]), TO_X3)
    total, gene_3, gene_2 = total + got[:ROWS], got[ROWS : ROWS + 2048], got[ROWS + 2048 :]
    factor = GENES / total
    factors = jnp.concatenate([factor, send(factor, TO_CORE)]).reshape(DEPTH, 1)
    gene_n = jnp.where((x + core) % 2 == 0, gene_1, gene_3).reshape(2, 1024)
    own, gene_y, gene_2 = own.reshape(2, 1024), gene_y.reshape(2, 1024), gene_2.reshape(2, 1024)

    own_rows = row_groups(whole, whole_sib, factors, own, z)
    flip = lambda v, h: jnp.where(h == 0, v, jnp.concatenate([v[:, HALF:], v[:, :HALF]], axis=1))
    gene_n = flip(gene_n, core)
    cols_1 = column_chunks([(whole, whole_sib, own, core), (n0_mine, n0_sib, gene_n, 0)], factors)
    sa, sb, ka, kb = products([(0, 0, 0, 0), (0, 1, 0, 0), (0, 0, 0, 1), (0, 1, 0, 1)], [own_rows], [cols_1])
    ga, gb = send(sa, TO_Z1), send(sb, TO_Z3)
    x2_mine, x2_sib = send(n0_mine, TO_SAME), send(n0_sib, TO_SAME)
    y_sib = send(y_mine, TO_CORE)
    sa, sb, ka, kb = second(ka, kb, ga, gb)
    round_1 = (ka, kb, send(sa, TO_Z3), send(sb, TO_Z1))

    y_rows = row_groups(y_mine, y_sib, factors, gene_y, z)
    cols_2 = column_chunks([(n1_mine, n1_sib, gene_n[:, HALF:], 0)], factors)
    steps = [(1, 0, 0, 0), (1, 1, 0, 0), (1, 0, 0, 1), (1, 1, 0, 1), (0, 0, 1, 0), (0, 1, 1, 0), (1, 0, 1, 0), (1, 1, 1, 0)]
    sa, sb, ka, kb = products(steps, [own_rows, y_rows], [cols_1, cols_2])
    ga, gb = send(sa, TO_Z1), send(sb, TO_Z3)
    sa, sb, ka, kb = second(ka, kb, ga, gb)
    round_2 = (ka, kb, send(sa, TO_Z3), send(sb, TO_Z1))

    cols_3 = column_chunks([(x2_mine, x2_sib, flip(gene_2, core), 0)], factors)
    steps = [(0, 0, 0, 0), (0, 1, 0, 0), (1, 0, 0, 0), (1, 1, 0, 0)]
    sa, sb, ka, kb = products(steps, [own_rows, y_rows], [cols_3])
    ga, gb = send(sa, TO_Z1), send(sb, TO_Z3)
    sa, sb, ka, kb = second(ka, kb, ga, gb)
    round_3 = (ka, kb, send(sa, TO_Z3), send(sb, TO_Z1))

    away = (b ^ high).astype(jnp.int32)
    groups = jnp.stack([2 * (dy ^ away) + (core ^ dc) for dy in (0, 1) for dc in (0, 1)])
    tables = [
        [(0, 0), (0, 1), (1, 0), (1, 1)],
        [(0, 2), (0, 3), (1, 2), (1, 3)],
        [(1, 4), (1, 5), (1, 6), (1, 7)],
    ]
    keep, to_c, to_y, to_yc = summed_z([round_1, round_2], groups, tables)
    near = (x + 1 - 2 * core) % 4
    far = (x - 1 + 2 * core) % 4
    opposite = x ^ 2
    places = jnp.stack(
        [2 * x + core, 2 * near + core, 2 * near + 1 - core, 2 * x + 1 - core, 2 * far + 1 - core, 2 * far + core]
    ).astype(jnp.int32)
    out = finish(keep, send(to_c, TO_CORE), send(to_y, TO_YHI), send(to_yc, TO_YHI_CORE), places)
    keep, to_c, to_y, to_yc = summed_z([round_3], groups, [[(0, 0), (0, 1), (0, 2), (0, 3)]])
    places = jnp.stack([2 * opposite + core, 2 * opposite + 1 - core]).astype(jnp.int32)
    out = finish(keep, send(to_c, TO_CORE), send(to_y, TO_YHI), send(to_yc, TO_YHI_CORE), places, out)
    return out.reshape(1, 128, 1, 4, 1024)


def solution(mesh):
    placed = (P("cells", "grow", "gcol", None), P("grow", "gcol", None), P("grow", "gcol", None))
    return jax.shard_map(
        per_device,
        mesh=mesh,
        in_specs=placed,
        out_specs=P("grow", "cells", "gcol", None, None),
        check_vma=False,
    )
```

```python
import jax
import jax.numpy as jnp
import numpy as np
from jax import lax
from jax.experimental import pallas as pl
from jax.experimental.pallas import tpu as pltpu
from jax.sharding import PartitionSpec as P

GENES = 8192
CELLS = 18432
AXES = ("cells", "grow", "gcol")
SIZES = (2, 4, 2, 4, 2)
ROWS = 1152
TILES = ROWS // 128
SPAN = 1024
HALF = 512
QUARTER = 256

ALPHA = 2.0**17 / 9.0e6
BETA = 32700.0 / float(np.log1p(2.0**17))
VMEM = 48 * 1024 * 1024


def moves(target):
    pairs = []
    for i, at in enumerate(np.ndindex(*SIZES)):
        to = tuple(v % s for v, s in zip(target(*at), SIZES))
        pairs.append((i, int(np.ravel_multi_index(to, SIZES))))
    return pairs


TO_CORE = moves(lambda h, z, c, x, b: (h, z, 1 - c, x, b))
TO_YLO = moves(lambda h, z, c, x, b: (h, z, c, x, 1 - b))
TO_YHI = moves(lambda h, z, c, x, b: (1 - h, z, c, x, b))
TO_YHI_CORE = moves(lambda h, z, c, x, b: (1 - h, z, 1 - c, x, b))
TO_X = [moves(lambda h, z, c, x, b, d=d: (h, z, c, x + d, b)) for d in (1, 2, 3)]
FIRST = (1, 3)
TO_Z_FIRST = moves(lambda h, z, c, x, b: (h, z ^ FIRST[c], c, x, b))
TO_Z_SECOND = moves(lambda h, z, c, x, b: (h, z ^ FIRST[1 - c], c, x, b))
TO_SAME = moves(lambda h, z, c, x, b: (h, z, c, x - 1 + 2 * c, b))
TO_CROSS = moves(lambda h, z, c, x, b: (h, z, 1 - c, x + 1 - 2 * c, b))

CORE, AWAY, KEEP, SEND, PLACE = 0, 1, 2, 4, 6


def table():
    rows = []
    for h, z, c, x, b in np.ndindex(*SIZES):
        row = [c, b ^ h]
        row += [(z ^ d) * QUARTER for d in (0, FIRST[1 - c], FIRST[c], 2)]
        for core in (c, 1 - c):
            near = (x + 1 - 2 * core) % 4
            chunks = ((x, core), (near, core), (near, 1 - core), (x ^ 2, core))
            row += [half * 16 + a for a, half in chunks]
        rows.append(row + [0] * 2)
    return np.array(rows, np.int32)


def send(value, pairs):
    return lax.ppermute(value, AXES, pairs)


def encode(total):
    size = jnp.log(1.0 + ALPHA * jnp.abs(total)) * BETA + 0.5
    code = size.astype(jnp.int32)
    return jnp.where(total < 0, -code, code).astype(jnp.int16)


def decode(code):
    code = code.astype(jnp.int32).astype(jnp.float32)
    size = (jnp.exp(jnp.abs(code) * (1.0 / BETA)) - 1.0) * (1.0 / ALPHA)
    return jnp.where(code < 0, -size, size)


def params(**_):
    return dict(
        compiler_params=pltpu.CompilerParams(vmem_limit_bytes=VMEM),
        cost_estimate=pl.CostEstimate(flops=30_000_000_000, bytes_accessed=1_000_000, transcendentals=0),
    )


def of(shape, dtype):
    return jax.ShapeDtypeStruct(shape, dtype)


STEPS = 3
PART = ROWS // STEPS
PART_TILES = PART // 128


def sums(counts, mean, scale):
    def body(counts_ref, mean_ref, scale_ref, out_ref):
        i = pl.program_id(0)

        @pl.when(i == 0)
        def _():
            inverse = 1.0 / scale_ref[...]
            out_ref[TILES : TILES + 8, :] = inverse
            out_ref[TILES + 8 : TILES + 16, :] = mean_ref[...] * inverse

        total = None
        for j in range(8):
            value = counts_ref[pl.ds(j, PART, stride=8), :]
            total = value if total is None else total + value
        total = total.astype(jnp.float32)
        for k in range(PART_TILES):
            across = jnp.sum(total[k * 128 : (k + 1) * 128, :].T, axis=0, keepdims=True)
            out_ref[pl.ds(i * PART_TILES + k, 1), :] = across

    whole = pl.BlockSpec((8, 128), lambda i: (0, 0))
    return pl.pallas_call(
        body,
        out_shape=of((TILES + 16, 128), jnp.float32),
        grid=(STEPS,),
        in_specs=[pl.BlockSpec((PART * 8, 128), lambda i: (i, 0)), whole, whole],
        out_specs=pl.BlockSpec((TILES + 16, 128), lambda i: (0, 0)),
        **params(byte=5 << 20),
    )(counts, mean, scale)


def narrow(counts, after):
    def body(counts_ref, after_ref, out_ref):
        for j in range(8):
            out_ref[:, j * 128 : (j + 1) * 128] = counts_ref[pl.ds(j, PART, stride=8), :].astype(jnp.int16)

    return pl.pallas_call(
        body,
        out_shape=of((ROWS, SPAN), jnp.int16),
        grid=(STEPS,),
        in_specs=[pl.BlockSpec((PART * 8, 128), lambda i: (i, 0)), pl.BlockSpec(memory_space=pl.ANY)],
        out_specs=pl.BlockSpec((PART, SPAN), lambda i: (i, 0)),
        **params(byte=8 << 20),
    )(counts, after)


def join(part, part_y, after):
    def body(part_ref, y_ref, after_ref, out_ref):
        out_ref[0:TILES, :] = part_ref[0:TILES, :] + y_ref[0:TILES, :]
        out_ref[TILES:, :] = part_ref[TILES:, :]

    small = pl.BlockSpec(memory_space=pltpu.VMEM)
    return pl.pallas_call(
        body,
        out_shape=of(part.shape, part.dtype),
        in_specs=[small, small, pl.BlockSpec(memory_space=pl.ANY)],
        out_specs=small,
        **params(),
    )(part, part_y, after)


def halves(where, block, after):
    def body(where_ref, first_in, other_in, after_ref, first_ref, other_ref):
        first_ref[...] = first_in[...]
        other_ref[...] = other_in[...]

    half = pl.BlockSpec((PART, HALF), lambda i, w: (i, 0))
    return pl.pallas_call(
        body,
        out_shape=(of((ROWS, HALF), block.dtype),) * 2,
        grid_spec=pltpu.PrefetchScalarGridSpec(
            num_scalar_prefetch=1,
            grid=(STEPS,),
            in_specs=[
                pl.BlockSpec((PART, HALF), lambda i, w: (i, w[CORE])),
                pl.BlockSpec((PART, HALF), lambda i, w: (i, 1 - w[CORE])),
                pl.BlockSpec(memory_space=pl.ANY),
            ],
            out_specs=[half, half],
        ),
        **params(byte=5 << 20),
    )(where, block, block, after)


def factors(total_refs, i):
    tiles = []
    for k in range(PART_TILES):
        row = sum(ref[pl.ds(i * PART_TILES + k, 1), :] for ref in total_refs)
        tiles.append(jnp.broadcast_to(GENES / row, (128, 128)).T)
    return jnp.concatenate(tiles, axis=0)


def standardized(count, factor, inverse, shift):
    value = count.astype(jnp.int32).astype(jnp.float32)
    return (jnp.log(1.0 + value * factor) * inverse - shift).astype(jnp.bfloat16)


SMALL = (TILES + 16, 128)


def standardize(where, counts, totals, gene, after, split):
    n = len(totals)

    def body(where_ref, counts_ref, *refs):
        gene_ref, after_ref, out_ref = refs[n : n + 3]
        half = pl.program_id(1)
        factor = factors(refs[:n], pl.program_id(0))

        def run(*out_refs):
            for j in range(4):
                lanes = slice(j * 128, (j + 1) * 128)
                at = TILES + half * 4 + j
                inverse, shift = gene_ref[pl.ds(at, 1), :], gene_ref[pl.ds(at + 8, 1), :]
                value = standardized(counts_ref[:, lanes], factor, inverse, shift)
                for ref in out_refs:
                    ref[:, lanes] = value

        if split:
            first_ref, other_ref = refs[n + 3 :]

            @pl.when(half == where_ref[CORE])
            def _():
                run(out_ref, first_ref)

            @pl.when(half != where_ref[CORE])
            def _():
                run(out_ref, other_ref)

        else:
            run(out_ref)

    small = pl.BlockSpec(SMALL, lambda i, h, w: (0, 0))
    rows = pl.BlockSpec((TILES, 128), lambda i, h, w: (0, 0))
    block = pl.BlockSpec((PART, HALF), lambda i, h, w: (i, h))
    half = pl.BlockSpec((PART, HALF), lambda i, h, w: (i, 0))
    whole = of((ROWS, SPAN), jnp.bfloat16)
    halved = (of((ROWS, HALF), jnp.bfloat16),) * 2
    return pl.pallas_call(
        body,
        out_shape=(whole, *halved) if split else whole,
        grid_spec=pltpu.PrefetchScalarGridSpec(
            num_scalar_prefetch=1,
            grid=(STEPS, 2),
            in_specs=[block] + [rows] * n + [small] + [pl.BlockSpec(memory_space=pl.ANY)],
            out_specs=[block, half, half] if split else block,
        ),
        **params(byte=7 << 20),
    )(where, counts, *totals, gene, after)


def standardize_near(where, mine, sibling, total, total_sibling, right, left):
    def body(where_ref, mine_ref, sibling_ref, t_ref, ts_ref, right_ref, left_ref, out_ref):
        i = pl.program_id(0)
        core = where_ref[CORE]

        def run(count_ref, total_ref, gene_ref):
            factor = factors([total_ref], i % STEPS)
            for j in range(4):
                lanes = slice(j * 128, (j + 1) * 128)
                at = TILES + core * 4 + j
                inverse, shift = gene_ref[pl.ds(at, 1), :], gene_ref[pl.ds(at + 8, 1), :]
                out_ref[:, lanes] = standardized(count_ref[:, lanes], factor, inverse, shift)

        for part, count_ref, total_ref in ((0, mine_ref, t_ref), (1, sibling_ref, ts_ref)):
            for side, gene_ref in ((0, right_ref), (1, left_ref)):

                @pl.when((i // STEPS == part) & (core == side))
                def _():
                    run(count_ref, total_ref, gene_ref)

    small = pl.BlockSpec(SMALL, lambda i, w: (0, 0))
    rows = pl.BlockSpec((TILES, 128), lambda i, w: (0, 0))
    return pl.pallas_call(
        body,
        out_shape=of((2 * ROWS, HALF), jnp.bfloat16),
        grid_spec=pltpu.PrefetchScalarGridSpec(
            num_scalar_prefetch=1,
            grid=(2 * STEPS,),
            in_specs=[
                pl.BlockSpec((PART, HALF), lambda i, w: (jnp.minimum(i, STEPS - 1), 0)),
                pl.BlockSpec((PART, HALF), lambda i, w: (jnp.maximum(i - STEPS, 0), 0)),
                rows,
                rows,
                small,
                small,
            ],
            out_specs=pl.BlockSpec((PART, HALF), lambda i, w: (i, 0)),
        ),
        **params(byte=5 << 20),
    )(where, mine, sibling, total, total_sibling, right, left)


def products(where, rows, cols, after):
    n_rows, n_cols = len(rows), len(cols)
    units = max(n_rows, n_cols)
    flat = [a for block in rows + cols for a in block]

    def body(where_ref, *refs):
        sources = refs[: len(flat)]
        go_ref, stay_ref, rows_v, cols_v, *product, sems = refs[len(flat) + 1 :]
        step = pl.program_id(0)
        core = where_ref[CORE]

        def copies(unit):
            which = []
            k = 0
            for b, block in enumerate(rows + cols):
                place, u = (rows_v, b) if b < n_rows else (cols_v, b - n_rows)
                for part in range(len(block)):
                    if u == unit:
                        source = sources[k]
                        size = source.shape[0]
                        if b >= n_rows and source.shape[1] == SPAN:
                            source = source.at[:, pl.ds(pl.multiple_of(core * HALF, HALF), HALF)]
                        target = place.at[u, pl.ds(part * size, size)]
                        which.append(pltpu.make_async_copy(source, target, sems.at[k]))
                    k += 1
            return which

        @pl.when(step == 0)
        def _():
            for unit in range(units):
                for c in copies(unit):
                    c.start()

        for unit in range(units):

            @pl.when(step == unit)
            def _():
                for c in copies(unit):
                    c.wait()

        r = step if n_rows > 1 else 0
        q = step if n_cols > 1 else 0
        for tile in range(2):
            lanes = slice(tile * 256, tile * 256 + 256)
            product[tile][...] = lax.dot_general(
                rows_v[r], cols_v[q, :, lanes], (((0,), (0,)), ((), ())), preferred_element_type=jnp.float32
            )
            for k in range(2):
                at = pl.multiple_of(where_ref[KEEP + k], QUARTER)
                stay_ref[0, k, :, lanes] = product[tile][pl.ds(at, QUARTER), :]
                at = pl.multiple_of(where_ref[SEND + k], QUARTER)
                go_ref[0, k, :, lanes] = encode(product[tile][pl.ds(at, QUARTER), :])

    out = pl.BlockSpec((1, 2, QUARTER, HALF), lambda i, w: (i, 0, 0, 0))
    return pl.pallas_call(
        body,
        out_shape=(of((units, 2, QUARTER, HALF), jnp.int16), of((units, 2, QUARTER, HALF), jnp.float32)),
        grid_spec=pltpu.PrefetchScalarGridSpec(
            num_scalar_prefetch=1,
            grid=(units,),
            in_specs=[pl.BlockSpec(memory_space=pltpu.HBM)] * len(flat) + [pl.BlockSpec(memory_space=pl.ANY)],
            out_specs=[out, out],
            scratch_shapes=[
                pltpu.VMEM((n_rows, 2 * ROWS, SPAN), jnp.bfloat16),
                pltpu.VMEM((n_cols, 2 * ROWS, HALF), jnp.bfloat16),
                pltpu.VMEM((SPAN, 256), jnp.float32),
                pltpu.VMEM((SPAN, 256), jnp.float32),
                pltpu.SemaphoreType.DMA((len(flat),)),
            ],
        ),
        **params(flops=2 * units * SPAN * HALF * 2 * ROWS, byte=6 * units << 20),
    )(where, *flat, after)


def second(stay, got):
    units = stay.shape[0]

    def body(stay_ref, got_ref, go_ref, out_ref):
        out_ref[0] = stay_ref[0, 0] + decode(got_ref[0, 0])
        go_ref[0] = encode(stay_ref[0, 1] + decode(got_ref[0, 1]))

    four = pl.BlockSpec((1, 2, QUARTER, HALF), lambda i: (i, 0, 0, 0))
    three = pl.BlockSpec((1, QUARTER, HALF), lambda i: (i, 0, 0))
    return pl.pallas_call(
        body,
        grid=(units,),
        out_shape=(of((units, QUARTER, HALF), jnp.int16), of((units, QUARTER, HALF), jnp.float32)),
        in_specs=[four, four],
        out_specs=[three, three],
        **params(byte=5 << 20),
    )(stay, got)


def summed_z(where, chunks, own, other):
    parts = own + other

    def body(where_ref, *refs):
        keep, to_c, to_y, to_yc, total = refs[2 * len(parts) :]
        i = pl.program_id(0)
        for p, (_, _, which) in enumerate(parts):
            held = [k for k in range(chunks) if which[k] is not None]
            side = 0 if p < len(own) else 1

            @pl.when((i >= held[0]) & (i <= held[-1]))
            def _():
                total[side] = refs[2 * p][0] + decode(refs[2 * p + 1][0])

        near, far = where_ref[AWAY], 1 - where_ref[AWAY]
        mine = pl.ds(pl.multiple_of(where_ref[CORE] * 128, 128), 128)
        others = pl.ds(pl.multiple_of((1 - where_ref[CORE]) * 128, 128), 128)
        keep[0] = total[near, mine, :]
        to_c[0] = encode(total[near, others, :])
        to_y[0] = encode(total[far, mine, :])
        to_yc[0] = encode(total[far, others, :])

    def at(which):
        held = [(k, u) for k, u in enumerate(which) if u is not None]
        first, base = held[0]
        return lambda i, w: (jnp.clip(i - first, 0, len(held) - 1) + base, 0, 0)

    in_specs, operands = [], []
    for stay, got, which in parts:
        in_specs += [pl.BlockSpec((1, QUARTER, HALF), at(which))] * 2
        operands += [stay, got]
    return pl.pallas_call(
        body,
        out_shape=(of((chunks, 128, HALF), jnp.float32),) + (of((chunks, 128, HALF), jnp.int16),) * 3,
        grid_spec=pltpu.PrefetchScalarGridSpec(
            num_scalar_prefetch=1,
            grid=(chunks,),
            in_specs=in_specs,
            out_specs=[pl.BlockSpec((1, 128, HALF), lambda i, w: (i, 0, 0))] * 4,
            scratch_shapes=[pltpu.VMEM((2, QUARTER, HALF), jnp.float32)],
        ),
        **params(byte=chunks * (2 << 20)),
    )(where, *operands)


def finish(where, keep, got_c, got_y, got_yc, chunk, out=None):
    n = keep.shape[0]

    def body(where_ref, keep_ref, c_ref, y_ref, yc_ref, *rest):
        out_ref = rest[-1]
        i = pl.program_id(0)
        if out is not None:

            @pl.when(i == 0)
            def _():
                out_ref[...] = rest[0][...]

        mine = (keep_ref[0] + decode(y_ref[0])) * (1.0 / CELLS)
        others = (decode(c_ref[0]) + decode(yc_ref[0])) * (1.0 / CELLS)
        for place, value in ((PLACE, mine), (PLACE + 4, others)):
            base = where_ref[place + chunk + i]
            for q in range(4):
                out_ref[pl.ds(base + 4 * q, 128, stride=32), :] = value[:, q * 128 : (q + 1) * 128]

    block = pl.BlockSpec((1, 128, HALF), lambda i, w: (i, 0, 0))
    whole = pl.BlockSpec((4096, 128), lambda i, w: (0, 0))
    in_specs, operands, alias = [block] * 4, [keep, got_c, got_y, got_yc], {}
    if out is not None:
        in_specs.append(whole)
        operands.append(out)
        alias = {5: 0}
    return pl.pallas_call(
        body,
        out_shape=of((4096, 128), jnp.float32),
        grid_spec=pltpu.PrefetchScalarGridSpec(
            num_scalar_prefetch=1, grid=(n,), in_specs=in_specs, out_specs=whole
        ),
        input_output_aliases=alias,
        **params(byte=4 << 20),
    )(where, *operands)


def exchange_z(go, stay):
    go, stay = second(stay, send(go, TO_Z_FIRST))
    return stay, send(go, TO_Z_SECOND)


def per_device(counts, gene_mean, gene_scale):
    device = (lax.axis_index("cells") * 4 + lax.axis_index("grow")) * 2 + lax.axis_index("gcol")
    where = lax.dynamic_slice(jnp.asarray(table()), (device, 0), (1, 16)).reshape(16)
    counts = counts.reshape(ROWS * 8, 128)

    part = sums(counts, gene_mean.reshape(8, 128), gene_scale.reshape(8, 128))
    part_y = send(part, TO_YLO)
    whole = narrow(counts, part)
    y_counts = send(whole, TO_YLO)
    pair = join(part, part_y, whole)
    left, opposite, right = [send(pair, to) for to in TO_X]
    first, other = halves(where, whole, pair)
    n0 = send(first, TO_SAME), send(other, TO_CROSS)
    total = pair[:TILES] + left[:TILES] + opposite[:TILES] + right[:TILES]
    total_sibling = send(total, TO_CORE)

    own, first, other = standardize(where, whole, [total], part, total, True)
    own = own, send(own, TO_CORE)
    n1 = send(other, TO_SAME), send(first, TO_CROSS)
    n0 = (standardize_near(where, *n0, total, total_sibling, right, left),)
    x2 = (send(n0[0], TO_SAME),)

    go, stay = products(where, [own], [own, n0], total)
    round_1 = exchange_z(go, stay)
    go, stay = products(where, [own], [n1], go)
    round_2 = exchange_z(go, stay)
    y = standardize(where, y_counts, [total], part_y, go, False)
    y = y, send(y, TO_CORE)
    go, stay = products(where, [y], [own, n0, n1], go)
    round_3 = exchange_z(go, stay)
    go, stay = products(where, [own, y], [x2], go)
    round_4 = exchange_z(go, stay)

    keep, to_c, to_y, to_yc = summed_z(
        where,
        3,
        [(*round_1, [0, 1, None]), (*round_2, [None, None, 0])],
        [(*round_3, [0, 1, 2])],
    )
    out = finish(where, keep, send(to_c, TO_CORE), send(to_y, TO_YHI), send(to_yc, TO_YHI_CORE), 0)
    keep, to_c, to_y, to_yc = summed_z(where, 1, [(*round_4, [0])], [(*round_4, [1])])
    out = finish(where, keep, send(to_c, TO_CORE), send(to_y, TO_YHI), send(to_yc, TO_YHI_CORE), 3, out)
    return out.reshape(128, 8, 4, 128).transpose(0, 2, 1, 3).reshape(1, 128, 1, 4, SPAN)


def solution(mesh):
    placed = (P("cells", "grow", "gcol", None), P("grow", "gcol", None), P("grow", "gcol", None))
    return jax.shard_map(
        per_device,
        mesh=mesh,
        in_specs=placed,
        out_specs=P("grow", "cells", "gcol", None, None),
        check_vma=False,
    )
```

```python
import jax
import jax.numpy as jnp
import numpy as np
from jax import lax
from jax.experimental import pallas as pl
from jax.experimental.pallas import tpu as pltpu
from jax.sharding import PartitionSpec as P

GENES = 8192
CELLS = 18432
AXES = ("cells", "grow", "gcol")
SIZES = (2, 4, 2, 4, 2)
ROWS = 1152
TILES = ROWS // 128
SPAN = 1024
HALF = 512
QUARTER = 256

ALPHA = 2.0**17 / 9.0e6
BETA = 32700.0 / float(np.log1p(2.0**17))
VMEM = 16 * 1024 * 1024
STREAMED = 58 * 1024 * 1024


def moves(target):
    pairs = []
    for i, at in enumerate(np.ndindex(*SIZES)):
        to = tuple(v % s for v, s in zip(target(*at), SIZES))
        pairs.append((i, int(np.ravel_multi_index(to, SIZES))))
    return pairs


TO_CORE = moves(lambda h, z, c, x, b: (h, z, 1 - c, x, b))
TO_YLO = moves(lambda h, z, c, x, b: (h, z, c, x, 1 - b))
TO_YHI = moves(lambda h, z, c, x, b: (1 - h, z, c, x, b))
TO_YHI_CORE = moves(lambda h, z, c, x, b: (1 - h, z, 1 - c, x, b))
TO_X = [moves(lambda h, z, c, x, b, d=d: (h, z, c, x + d, b)) for d in (1, 2, 3)]
FIRST = (1, 3)
TO_Z_FIRST = moves(lambda h, z, c, x, b: (h, z ^ FIRST[c], c, x, b))
TO_Z_SECOND = moves(lambda h, z, c, x, b: (h, z ^ FIRST[1 - c], c, x, b))
TO_SAME = moves(lambda h, z, c, x, b: (h, z, c, x - 1 + 2 * c, b))
TO_CROSS = moves(lambda h, z, c, x, b: (h, z, 1 - c, x + 1 - 2 * c, b))

def here():
    cells = lax.axis_index("cells")
    return cells >> 3, (cells >> 1) & 3, cells & 1, lax.axis_index("grow"), lax.axis_index("gcol")


def z_rows():
    _, z, core, _, _ = here()
    return [(z ^ d) * QUARTER for d in (0, 3 - 2 * core)], [(z ^ d) * QUARTER for d in (1 + 2 * core, 2)]


def out_place(chunk, other):
    _, _, core, x, _ = here()
    core = 1 - core if other else core
    near = (x + 1 - 2 * core) & 3
    block, half = ((x, core), (near, core), (near, 1 - core), (x ^ 2, core))[chunk]
    return half * 16 + block


def send(value, pairs):
    return lax.ppermute(value, AXES, pairs)


def encode(total):
    size = jnp.log(1.0 + ALPHA * jnp.abs(total)) * BETA + 0.5
    code = size.astype(jnp.int32)
    return jnp.where(total < 0, -code, code).astype(jnp.int16)


def decode(code):
    code = code.astype(jnp.int32).astype(jnp.float32)
    size = (jnp.exp(jnp.abs(code) * (1.0 / BETA)) - 1.0) * (1.0 / ALPHA)
    return jnp.where(code < 0, -size, size)


def params(vmem=VMEM):
    return dict(
        compiler_params=pltpu.CompilerParams(vmem_limit_bytes=vmem),
        cost_estimate=pl.CostEstimate(flops=30_000_000_000, bytes_accessed=1_000_000, transcendentals=0),
    )


HELD = pl.BlockSpec(memory_space=pltpu.VMEM)
LOOSE = pl.BlockSpec()
ANYWHERE = pl.BlockSpec(memory_space=pl.ANY)


def of(shape, dtype):
    return jax.ShapeDtypeStruct(shape, dtype)


STEPS = 3
PART = ROWS // STEPS
PART_TILES = PART // 128


def take(counts, mean, scale):
    def body(counts_ref, mean_ref, scale_ref, out_ref, narrow_ref, counts_v, mean_v, scale_v, sems):
        parts = []
        for i in range(STEPS):
            rows = pl.ds(i * PART * 8, PART * 8)
            parts.append(pltpu.make_async_copy(counts_ref.at[rows], counts_v.at[rows], sems.at[i]))
        genes = [
            pltpu.make_async_copy(mean_ref, mean_v, sems.at[STEPS]),
            pltpu.make_async_copy(scale_ref, scale_v, sems.at[STEPS + 1]),
        ]
        for c in parts + genes:
            c.start()
        for i in range(STEPS):
            parts[i].wait()
            total = None
            for j in range(8):
                value = counts_v[pl.ds(i * PART * 8 + j, PART, stride=8), :]
                narrow_ref[i * PART : (i + 1) * PART, j * 128 : (j + 1) * 128] = value.astype(jnp.int16)
                total = value if total is None else total + value
            total = total.astype(jnp.float32)
            for k in range(PART_TILES):
                across = jnp.sum(total[k * 128 : (k + 1) * 128, :].T, axis=0, keepdims=True)
                out_ref[i * PART_TILES + k : i * PART_TILES + k + 1, :] = across
        for c in genes:
            c.wait()
        inverse = 1.0 / scale_v[...]
        out_ref[TILES : TILES + 8, :] = inverse
        out_ref[TILES + 8 : TILES + 16, :] = mean_v[...] * inverse

    return pl.pallas_call(
        body,
        out_shape=(of((TILES + 16, 128), jnp.float32), of((ROWS, SPAN), jnp.int16)),
        in_specs=[pl.BlockSpec(memory_space=pltpu.HBM)] * 3,
        out_specs=(HELD, HELD),
        scratch_shapes=[
            pltpu.VMEM((ROWS * 8, 128), jnp.int32),
            pltpu.VMEM((8, 128), jnp.float32),
            pltpu.VMEM((8, 128), jnp.float32),
            pltpu.SemaphoreType.DMA((STEPS + 2,)),
        ],
        **params(STREAMED),
    )(counts, mean, scale)


def gate(arrays, after):
    n = len(arrays)
    return pl.pallas_call(
        lambda *refs: None,
        out_shape=tuple(of(a.shape, a.dtype) for a in arrays),
        in_specs=[pl.BlockSpec(memory_space=pl.ANY)] * (n + 1),
        out_specs=[pl.BlockSpec(memory_space=pl.ANY)] * n,
        input_output_aliases={k: k for k in range(n)},
        **params(),
    )(*arrays, after)


def join(part, part_y, after):
    def body(part_ref, y_ref, after_ref, out_ref):
        out_ref[0:TILES, :] = part_ref[0:TILES, :] + y_ref[0:TILES, :]
        out_ref[TILES:, :] = part_ref[TILES:, :]

    return pl.pallas_call(
        body,
        out_shape=of(part.shape, part.dtype),
        in_specs=[HELD, HELD, ANYWHERE],
        out_specs=HELD,
        **params(),
    )(part, part_y, after)


def halves(block, after):
    def body(block_ref, after_ref, first_ref, other_ref):
        _, _, core, _, _ = here()

        def run(low_ref, high_ref):
            def tile(at):
                rows = pl.ds(at, 128)
                low_ref[rows, :] = block_ref[rows, 0:HALF]
                high_ref[rows, :] = block_ref[rows, HALF:SPAN]

            by_tiles(tile)

        @pl.when(core == 0)
        def _():
            run(first_ref, other_ref)

        @pl.when(core != 0)
        def _():
            run(other_ref, first_ref)

    return pl.pallas_call(
        body,
        out_shape=(of((ROWS, HALF), block.dtype),) * 2,
        in_specs=[HELD, ANYWHERE],
        out_specs=(HELD, HELD),
        **params(),
    )(block, after)


def spread(total_refs, factor_v):
    for k in range(TILES):
        row = sum(ref[k : k + 1, :] for ref in total_refs)
        factor_v[k * 128 : (k + 1) * 128, :] = jnp.broadcast_to(GENES / row, (128, 128)).T


def standardized(count, factor, inverse, shift):
    value = count.astype(jnp.int32).astype(jnp.float32)
    return (jnp.log(1.0 + value * factor) * inverse - shift).astype(jnp.bfloat16)


def by_tiles(run):
    def step(t, carry):
        run(pl.multiple_of(t * 128, 128))
        return carry

    lax.fori_loop(0, TILES, step, 0)


def standardize(counts, total, gene, after):
    def body(counts_ref, total_ref, gene_ref, after_ref, out_ref, factor_v):
        spread([total_ref], factor_v)

        def tile(at):
            rows = pl.ds(at, 128)
            factor = factor_v[rows, :]
            for j in range(8):
                lanes = slice(j * 128, (j + 1) * 128)
                inverse, shift = gene_ref[TILES + j : TILES + j + 1, :], gene_ref[TILES + 8 + j : TILES + 9 + j, :]
                out_ref[rows, lanes] = standardized(counts_ref[rows, lanes], factor, inverse, shift)

        by_tiles(tile)

    return pl.pallas_call(
        body,
        out_shape=of((ROWS, SPAN), jnp.bfloat16),
        in_specs=[HELD, HELD, HELD, ANYWHERE],
        out_specs=HELD,
        scratch_shapes=[pltpu.VMEM((ROWS, 128), jnp.float32)],
        **params(),
    )(counts, total, gene, after)


def mark(after):
    def body(after_ref, out_ref):
        out_ref[...] = jnp.zeros((8, 128), jnp.float32)

    return pl.pallas_call(
        body, out_shape=of((8, 128), jnp.float32), in_specs=[ANYWHERE], out_specs=HELD, **params()
    )(after)


def other_half(mine, sibling, *after):
    def body(mine_ref, sibling_ref, *rest):
        out_ref = rest[-1]
        _, _, core, _, _ = here()

        def run(lanes):
            def tile(at):
                out_ref[pl.ds(at, 128), :] = mine_ref[pl.ds(at, 128), lanes]
                out_ref[pl.ds(at + ROWS, 128), :] = sibling_ref[pl.ds(at, 128), lanes]

            by_tiles(tile)

        @pl.when(core == 0)
        def _():
            run(slice(HALF, SPAN))

        @pl.when(core != 0)
        def _():
            run(slice(0, HALF))

    return pl.pallas_call(
        body,
        out_shape=of((2 * ROWS, HALF), mine.dtype),
        in_specs=[HELD, HELD] + [ANYWHERE] * len(after),
        out_specs=HELD,
        **params(),
    )(mine, sibling, *after)


def standardize_near(mine, sibling, total, total_sibling, right, left, after):
    def body(mine_ref, sibling_ref, t_ref, ts_ref, right_ref, left_ref, after_ref, out_ref, factor_v, gene_v):
        _, _, core, _, _ = here()
        gene_v[...] = jnp.where(core == 0, right_ref[...], left_ref[...])
        for part, count_ref, total_ref in ((0, mine_ref, t_ref), (1, sibling_ref, ts_ref)):
            spread([total_ref], factor_v)

            def tile(at, part=part, count_ref=count_ref):
                factor = factor_v[pl.ds(at, 128), :]
                for j in range(4):
                    lanes = slice(j * 128, (j + 1) * 128)
                    g = TILES + core * 4 + j
                    inverse, shift = gene_v[pl.ds(g, 1), :], gene_v[pl.ds(g + 8, 1), :]
                    out_ref[pl.ds(at + part * ROWS, 128), lanes] = standardized(
                        count_ref[pl.ds(at, 128), lanes], factor, inverse, shift
                    )

            by_tiles(tile)

    return pl.pallas_call(
        body,
        out_shape=of((2 * ROWS, HALF), jnp.bfloat16),
        in_specs=[HELD] * 6 + [ANYWHERE],
        out_specs=HELD,
        scratch_shapes=[pltpu.VMEM((ROWS, 128), jnp.float32), pltpu.VMEM((TILES + 16, 128), jnp.float32)],
        **params(),
    )(mine, sibling, total, total_sibling, right, left, after)


def products(rows, cols, after):
    n_rows, n_cols = len(rows), len(cols)
    units = max(n_rows, n_cols)
    flat = [a for block in rows + cols for a in block]

    def body(*refs):
        go_ref, stay_ref = refs[len(flat) + len(after) :]
        _, _, core, _, _ = here()
        stays, goes = z_rows()
        blocks, k = [], 0
        for block in rows + cols:
            blocks.append(refs[k : k + len(block)])
            k += len(block)

        def right(col, part):
            if len(col) == 1:
                return col[0][part * ROWS : (part + 1) * ROWS, :]
            if col[part].shape[1] == SPAN:
                return col[part][:, pl.ds(pl.multiple_of(core * HALF, HALF), HALF)]
            return col[part][...]

        for unit in range(units):
            row = blocks[unit if n_rows > 1 else 0]
            col = blocks[n_rows + (unit if n_cols > 1 else 0)]

            def product(at):
                at = pl.multiple_of(at, QUARTER)
                terms = [
                    lax.dot_general(
                        row[part][:, pl.ds(at, QUARTER)],
                        right(col, part),
                        (((0,), (0,)), ((), ())),
                        preferred_element_type=jnp.float32,
                    )
                    for part in range(2)
                ]
                return terms[0] + terms[1]

            for k in range(2):
                go_ref[unit, k] = encode(product(goes[k]))
            for k in range(2):
                stay_ref[unit, k] = product(stays[k])

    return pl.pallas_call(
        body,
        out_shape=(of((units, 2, QUARTER, HALF), jnp.int16), of((units, 2, QUARTER, HALF), jnp.float32)),
        in_specs=[HELD] * len(flat) + [ANYWHERE] * len(after),
        out_specs=(HELD, HELD),
        **params(),
    )(*flat, *after)


def second(stay, got, after):
    units = stay.shape[0]

    def body(stay_ref, got_ref, after_ref, go_ref, out_ref):
        for u in range(units):
            go_ref[u] = encode(stay_ref[u, 1] + decode(got_ref[u, 1]))
            out_ref[u] = stay_ref[u, 0] + decode(got_ref[u, 0])

    return pl.pallas_call(
        body,
        out_shape=(of((units, QUARTER, HALF), jnp.int16), of((units, QUARTER, HALF), jnp.float32)),
        in_specs=[LOOSE, LOOSE, ANYWHERE],
        out_specs=(LOOSE, LOOSE),
        **params(),
    )(stay, got, after)


def summed_z(own, other, after):
    chunks = len(own)
    arrays = []
    for stay, got, _ in own + other:
        if not any(stay is a for a in arrays):
            arrays += [stay, got]
    places = [next(i for i, a in enumerate(arrays) if a is stay) for stay, _, _ in own + other]

    def body(*refs):
        keep, to_c, to_y, to_yc, total = refs[len(arrays) + 1 :]
        high, _, core, _, low = here()
        away = high ^ low
        mine = pl.ds(pl.multiple_of(core * 128, 128), 128)
        others = pl.ds(pl.multiple_of((1 - core) * 128, 128), 128)
        for k in range(chunks):
            for side in range(2):
                n = side * chunks + k
                unit = (own + other)[n][2]
                total[k, side] = refs[places[n]][unit] + decode(refs[places[n] + 1][unit])
            to_y[k] = encode(total[k, 1 - away, mine, :])
            to_yc[k] = encode(total[k, 1 - away, others, :])
            to_c[k] = encode(total[k, away, others, :])
            keep[k] = total[k, away, mine, :]

    return pl.pallas_call(
        body,
        out_shape=(of((chunks, 128, HALF), jnp.float32),) + (of((chunks, 128, HALF), jnp.int16),) * 3,
        in_specs=[LOOSE] * len(arrays) + [ANYWHERE],
        out_specs=(LOOSE,) * 4,
        scratch_shapes=[pltpu.VMEM((chunks, 2, QUARTER, HALF), jnp.float32)],
        **params(),
    )(*arrays, after)


def finish(parts, after, out=None):
    rows = 32
    flat = [a for part in parts for a in part[1:]]

    def body(*refs):
        out_ref = refs[-1]

        def step(i, carry):
            at = pl.ds(pl.multiple_of(i * rows, rows), rows)
            if out is not None:
                held = pl.ds(pl.multiple_of(i * rows * 32, rows * 32), rows * 32)
                out_ref[held, :] = refs[len(flat)][held, :]
            for p, part in enumerate(parts):
                keep_ref, c_ref, y_ref, yc_ref = refs[4 * p : 4 * p + 4]
                for k in range(part[1].shape[0]):
                    mine = (keep_ref[k, at, :] + decode(y_ref[k, at, :])) * (1.0 / CELLS)
                    others = (decode(c_ref[k, at, :]) + decode(yc_ref[k, at, :])) * (1.0 / CELLS)
                    for other, value in ((False, mine), (True, others)):
                        base = i * (rows * 32) + out_place(part[0] + k, other)
                        for q in range(4):
                            out_ref[pl.ds(base + 4 * q, rows, stride=32), :] = value[:, q * 128 : (q + 1) * 128]
            return carry

        lax.fori_loop(0, 128 // rows, step, 0)

    operands = flat if out is None else flat + [out]
    return pl.pallas_call(
        body,
        out_shape=of((4096, 128), jnp.float32),
        in_specs=[LOOSE] * len(flat) + ([] if out is None else [HELD]) + [ANYWHERE],
        out_specs=HELD,
        input_output_aliases={} if out is None else {len(flat): 0},
        **params(),
    )(*operands, after)


def shared(stay, to_c, to_y, to_yc):
    return stay, send(to_c, TO_CORE), send(to_y, TO_YHI), send(to_yc, TO_YHI_CORE)


def per_device(counts, gene_mean, gene_scale):
    counts = counts.reshape(ROWS * 8, 128)

    part, whole = take(counts, gene_mean.reshape(8, 128), gene_scale.reshape(8, 128))
    part_y = send(part, TO_YLO)
    (whole,) = gate([whole], part)
    y_counts = send(whole, TO_YLO)
    pair = join(part, part_y, whole)
    left, opposite, right = [send(pair, to) for to in TO_X]
    first, other = halves(whole, pair)
    n0 = send(first, TO_SAME), send(other, TO_CROSS)
    total = pair[:TILES] + left[:TILES] + opposite[:TILES] + right[:TILES]
    total_sibling = send(total, TO_CORE)

    own = standardize(whole, total, part, other)
    own = own, send(own, TO_CORE)
    n1 = other_half(*own, mark(own[0]), total_sibling)
    go_0, stay_0 = products([own], [own], [n1])
    n1 = (send(n1, TO_SAME),)
    got_0 = send(go_0, TO_Z_FIRST)
    n0 = (standardize_near(*n0, total, total_sibling, right, left, go_0),)
    x2 = (send(n0[0], TO_SAME),)
    go_1, stay_1 = products([own], [n0], [go_0])
    got_1 = send(go_1, TO_Z_FIRST)
    next_0, stay_0 = second(stay_0, got_0, go_1)
    round_0 = stay_0, send(next_0, TO_Z_SECOND)
    y = standardize(y_counts, total, part_y, next_0)
    y = y, send(y, TO_CORE)
    next_1, stay_1 = second(stay_1, got_1, y[0])
    round_1 = stay_1, send(next_1, TO_Z_SECOND)
    go_2, stay_2 = products([y], [own, n0], [next_1])
    got_2 = send(go_2, TO_Z_FIRST)
    go_3, stay_3 = products([own, y], [n1], [go_2])
    got_3 = send(go_3, TO_Z_FIRST)
    next_2, stay_2 = second(stay_2, got_2, go_3)
    round_2 = stay_2, send(next_2, TO_Z_SECOND)
    go_4, stay_4 = products([own, y], [x2], [next_2])
    got_4 = send(go_4, TO_Z_FIRST)
    next_3, stay_3 = second(stay_3, got_3, go_4)
    round_3 = stay_3, send(next_3, TO_Z_SECOND)
    sums_a = summed_z([(*round_0, 0), (*round_1, 0)], [(*round_2, 0), (*round_2, 1)], next_3)
    chunks_a = shared(*sums_a)
    next_4, stay_4 = second(stay_4, got_4, sums_a[0])
    round_4 = stay_4, send(next_4, TO_Z_SECOND)
    sums_b = summed_z([(*round_3, 0)], [(*round_3, 1)], next_4)
    chunks_b = shared(*sums_b)
    sums_c = summed_z([(*round_4, 0)], [(*round_4, 1)], sums_b[0])
    chunks_c = shared(*sums_c)
    out = finish([(0, *chunks_a), (2, *chunks_b)], sums_c[0])
    out = finish([(3, *chunks_c)], sums_c[0], out)
    return out.reshape(128, 8, 4, 128).transpose(0, 2, 1, 3).reshape(1, 128, 1, 4, SPAN)


def solution(mesh):
    placed = (P("cells", "grow", "gcol", None), P("grow", "gcol", None), P("grow", "gcol", None))
    return jax.shard_map(
        per_device,
        mesh=mesh,
        in_specs=placed,
        out_specs=P("grow", "cells", "gcol", None, None),
        check_vma=False,
    )
```

```python
import jax
import jax.numpy as jnp
import numpy as np
from jax import lax
from jax.experimental import pallas as pl
from jax.experimental.pallas import tpu as pltpu
from jax.sharding import PartitionSpec as P

GENES = 8192
CELLS = 18432
AXES = ("cells", "grow", "gcol")
SIZES = (2, 4, 2, 4, 2)
ROWS = 1152
TILES = ROWS // 128
SPAN = 1024
HALF = 512
QUARTER = 256

ALPHA = 2.0**17 / 9.0e6
BETA = 32700.0 / float(np.log1p(2.0**17))
VMEM = 16 * 1024 * 1024
STREAMED = 58 * 1024 * 1024


def moves(target):
    pairs = []
    for i, at in enumerate(np.ndindex(*SIZES)):
        to = tuple(v % s for v, s in zip(target(*at), SIZES))
        pairs.append((i, int(np.ravel_multi_index(to, SIZES))))
    return pairs


TO_CORE = moves(lambda h, z, c, x, b: (h, z, 1 - c, x, b))
TO_YLO = moves(lambda h, z, c, x, b: (h, z, c, x, 1 - b))
TO_YHI = moves(lambda h, z, c, x, b: (1 - h, z, c, x, b))
TO_YHI_CORE = moves(lambda h, z, c, x, b: (1 - h, z, 1 - c, x, b))
TO_X = [moves(lambda h, z, c, x, b, d=d: (h, z, c, x + d, b)) for d in (1, 2, 3)]
FIRST = (1, 3)
TO_Z_FIRST = moves(lambda h, z, c, x, b: (h, z ^ FIRST[c], c, x, b))
TO_Z_SECOND = moves(lambda h, z, c, x, b: (h, z ^ FIRST[1 - c], c, x, b))
TO_SAME = moves(lambda h, z, c, x, b: (h, z, c, x - 1 + 2 * c, b))
TO_CROSS = moves(lambda h, z, c, x, b: (h, z, 1 - c, x + 1 - 2 * c, b))

def here():
    cells = lax.axis_index("cells")
    return cells >> 3, (cells >> 1) & 3, cells & 1, lax.axis_index("grow"), lax.axis_index("gcol")


def z_rows():
    _, z, core, _, _ = here()
    return [(z ^ d) * QUARTER for d in (0, 3 - 2 * core)], [(z ^ d) * QUARTER for d in (1 + 2 * core, 2)]


def out_place(chunk, other):
    _, _, core, x, _ = here()
    core = 1 - core if other else core
    near = (x + 1 - 2 * core) & 3
    block, half = ((x, core), (near, core), (near, 1 - core), (x ^ 2, core))[chunk]
    return half * 16 + block


def send(value, pairs):
    return lax.ppermute(value, AXES, pairs)


def encode(total):
    size = jnp.log(1.0 + ALPHA * jnp.abs(total)) * BETA + 0.5
    code = size.astype(jnp.int32)
    return jnp.where(total < 0, -code, code).astype(jnp.int16)


def decode(code):
    code = code.astype(jnp.int32).astype(jnp.float32)
    size = (jnp.exp(jnp.abs(code) * (1.0 / BETA)) - 1.0) * (1.0 / ALPHA)
    return jnp.where(code < 0, -size, size)


def params(vmem=VMEM):
    return dict(
        compiler_params=pltpu.CompilerParams(vmem_limit_bytes=vmem),
        cost_estimate=pl.CostEstimate(flops=30_000_000_000, bytes_accessed=1_000_000, transcendentals=0),
    )


HELD = pl.BlockSpec(memory_space=pltpu.VMEM)
LOOSE = pl.BlockSpec()
ANYWHERE = pl.BlockSpec(memory_space=pl.ANY)


def of(shape, dtype):
    return jax.ShapeDtypeStruct(shape, dtype)


STEPS = 3
PART = ROWS // STEPS
PART_TILES = PART // 128


def take(counts, mean, scale):
    def body(counts_ref, mean_ref, scale_ref, out_ref, narrow_ref, counts_v, mean_v, scale_v, sems):
        parts = []
        for i in range(STEPS):
            rows = pl.ds(i * PART * 8, PART * 8)
            parts.append(pltpu.make_async_copy(counts_ref.at[rows], counts_v.at[rows], sems.at[i]))
        genes = [
            pltpu.make_async_copy(mean_ref, mean_v, sems.at[STEPS]),
            pltpu.make_async_copy(scale_ref, scale_v, sems.at[STEPS + 1]),
        ]
        for c in parts + genes:
            c.start()
        for i in range(STEPS):
            parts[i].wait()
            total = None
            for j in range(8):
                value = counts_v[pl.ds(i * PART * 8 + j, PART, stride=8), :]
                narrow_ref[i * PART : (i + 1) * PART, j * 128 : (j + 1) * 128] = value.astype(jnp.int16)
                total = value if total is None else total + value
            total = total.astype(jnp.float32)
            for k in range(PART_TILES):
                across = jnp.sum(total[k * 128 : (k + 1) * 128, :].T, axis=0, keepdims=True)
                out_ref[i * PART_TILES + k : i * PART_TILES + k + 1, :] = across
        for c in genes:
            c.wait()
        inverse = 1.0 / scale_v[...]
        out_ref[TILES : TILES + 8, :] = inverse
        out_ref[TILES + 8 : TILES + 16, :] = mean_v[...] * inverse

    return pl.pallas_call(
        body,
        out_shape=(of((TILES + 16, 128), jnp.float32), of((ROWS, SPAN), jnp.int16)),
        in_specs=[pl.BlockSpec(memory_space=pltpu.HBM)] * 3,
        out_specs=(HELD, HELD),
        scratch_shapes=[
            pltpu.VMEM((ROWS * 8, 128), jnp.int32),
            pltpu.VMEM((8, 128), jnp.float32),
            pltpu.VMEM((8, 128), jnp.float32),
            pltpu.SemaphoreType.DMA((STEPS + 2,)),
        ],
        **params(STREAMED),
    )(counts, mean, scale)


def gate(arrays, after):
    n = len(arrays)
    return pl.pallas_call(
        lambda *refs: None,
        out_shape=tuple(of(a.shape, a.dtype) for a in arrays),
        in_specs=[pl.BlockSpec(memory_space=pl.ANY)] * (n + 1),
        out_specs=[pl.BlockSpec(memory_space=pl.ANY)] * n,
        input_output_aliases={k: k for k in range(n)},
        **params(),
    )(*arrays, after)


def join(part, part_y, after):
    def body(part_ref, y_ref, after_ref, out_ref):
        out_ref[0:TILES, :] = part_ref[0:TILES, :] + y_ref[0:TILES, :]
        out_ref[TILES:, :] = part_ref[TILES:, :]

    return pl.pallas_call(
        body,
        out_shape=of(part.shape, part.dtype),
        in_specs=[HELD, HELD, ANYWHERE],
        out_specs=HELD,
        **params(),
    )(part, part_y, after)


def halves(block, after):
    def body(block_ref, after_ref, first_ref, other_ref):
        _, _, core, _, _ = here()

        def run(low_ref, high_ref):
            def tile(at):
                rows = pl.ds(at, 128)
                low_ref[rows, :] = block_ref[rows, 0:HALF]
                high_ref[rows, :] = block_ref[rows, HALF:SPAN]

            by_tiles(tile)

        @pl.when(core == 0)
        def _():
            run(first_ref, other_ref)

        @pl.when(core != 0)
        def _():
            run(other_ref, first_ref)

    return pl.pallas_call(
        body,
        out_shape=(of((ROWS, HALF), block.dtype),) * 2,
        in_specs=[HELD, ANYWHERE],
        out_specs=(HELD, HELD),
        **params(),
    )(block, after)


def spread(total_refs, factor_v):
    for k in range(TILES):
        row = sum(ref[k : k + 1, :] for ref in total_refs)
        factor_v[k * 128 : (k + 1) * 128, :] = jnp.broadcast_to(GENES / row, (128, 128)).T


def standardized(count, factor, inverse, shift):
    value = count.astype(jnp.int32).astype(jnp.float32)
    return (jnp.log(1.0 + value * factor) * inverse - shift).astype(jnp.bfloat16)


def by_tiles(run):
    def step(t, carry):
        run(pl.multiple_of(t * 128, 128))
        return carry

    lax.fori_loop(0, TILES, step, 0)


def standardize(counts, total, gene, after):
    def body(counts_ref, total_ref, gene_ref, after_ref, out_ref, factor_v):
        spread([total_ref], factor_v)

        def tile(at):
            rows = pl.ds(at, 128)
            factor = factor_v[rows, :]
            for j in range(8):
                lanes = slice(j * 128, (j + 1) * 128)
                inverse, shift = gene_ref[TILES + j : TILES + j + 1, :], gene_ref[TILES + 8 + j : TILES + 9 + j, :]
                out_ref[rows, lanes] = standardized(counts_ref[rows, lanes], factor, inverse, shift)

        by_tiles(tile)

    return pl.pallas_call(
        body,
        out_shape=of((ROWS, SPAN), jnp.bfloat16),
        in_specs=[HELD, HELD, HELD, ANYWHERE],
        out_specs=HELD,
        scratch_shapes=[pltpu.VMEM((ROWS, 128), jnp.float32)],
        **params(),
    )(counts, total, gene, after)


def mark(after):
    def body(after_ref, out_ref):
        out_ref[...] = jnp.zeros((8, 128), jnp.float32)

    return pl.pallas_call(
        body, out_shape=of((8, 128), jnp.float32), in_specs=[ANYWHERE], out_specs=HELD, **params()
    )(after)


def other_half(mine, sibling, *after):
    def body(mine_ref, sibling_ref, *rest):
        out_ref = rest[-1]
        _, _, core, _, _ = here()

        def run(lanes):
            def tile(at):
                out_ref[pl.ds(at, 128), :] = mine_ref[pl.ds(at, 128), lanes]
                out_ref[pl.ds(at + ROWS, 128), :] = sibling_ref[pl.ds(at, 128), lanes]

            by_tiles(tile)

        @pl.when(core == 0)
        def _():
            run(slice(HALF, SPAN))

        @pl.when(core != 0)
        def _():
            run(slice(0, HALF))

    return pl.pallas_call(
        body,
        out_shape=of((2 * ROWS, HALF), mine.dtype),
        in_specs=[HELD, HELD] + [ANYWHERE] * len(after),
        out_specs=HELD,
        **params(),
    )(mine, sibling, *after)


def standardize_near(mine, sibling, total, total_sibling, right, left, after):
    def body(mine_ref, sibling_ref, t_ref, ts_ref, right_ref, left_ref, after_ref, out_ref, copy_ref, factor_v, gene_v):
        _, _, core, _, _ = here()
        gene_v[...] = jnp.where(core == 0, right_ref[...], left_ref[...])
        for part, count_ref, total_ref in ((0, mine_ref, t_ref), (1, sibling_ref, ts_ref)):
            spread([total_ref], factor_v)

            def tile(at, part=part, count_ref=count_ref):
                factor = factor_v[pl.ds(at, 128), :]
                for j in range(4):
                    lanes = slice(j * 128, (j + 1) * 128)
                    g = TILES + core * 4 + j
                    inverse, shift = gene_v[pl.ds(g, 1), :], gene_v[pl.ds(g + 8, 1), :]
                    value = standardized(count_ref[pl.ds(at, 128), lanes], factor, inverse, shift)
                    out_ref[pl.ds(at + part * ROWS, 128), lanes] = value
                    copy_ref[pl.ds(at + part * ROWS, 128), lanes] = value

            by_tiles(tile)

    return pl.pallas_call(
        body,
        out_shape=(of((2 * ROWS, HALF), jnp.bfloat16),) * 2,
        in_specs=[HELD] * 6 + [ANYWHERE],
        out_specs=(HELD, HELD),
        scratch_shapes=[pltpu.VMEM((ROWS, 128), jnp.float32), pltpu.VMEM((TILES + 16, 128), jnp.float32)],
        **params(),
    )(mine, sibling, total, total_sibling, right, left, after)


def products(rows, cols, after):
    n_rows, n_cols = len(rows), len(cols)
    units = max(n_rows, n_cols)
    flat = [a for block in rows + cols for a in block]

    def body(*refs):
        go_ref, stay_ref = refs[len(flat) + len(after) :]
        _, _, core, _, _ = here()
        stays, goes = z_rows()
        blocks, k = [], 0
        for block in rows + cols:
            blocks.append(refs[k : k + len(block)])
            k += len(block)

        def right(col, part):
            if len(col) == 1:
                return col[0][part * ROWS : (part + 1) * ROWS, :]
            if col[part].shape[1] == SPAN:
                return col[part][:, pl.ds(pl.multiple_of(core * HALF, HALF), HALF)]
            return col[part][...]

        for unit in range(units):
            row = blocks[unit if n_rows > 1 else 0]
            col = blocks[n_rows + (unit if n_cols > 1 else 0)]

            def product(at):
                at = pl.multiple_of(at, QUARTER)
                terms = [
                    lax.dot_general(
                        row[part][:, pl.ds(at, QUARTER)],
                        right(col, part),
                        (((0,), (0,)), ((), ())),
                        preferred_element_type=jnp.float32,
                    )
                    for part in range(2)
                ]
                return terms[0] + terms[1]

            for k in range(2):
                go_ref[unit, k] = encode(product(goes[k]))
            for k in range(2):
                stay_ref[unit, k] = product(stays[k])

    return pl.pallas_call(
        body,
        out_shape=(of((units, 2, QUARTER, HALF), jnp.int16), of((units, 2, QUARTER, HALF), jnp.float32)),
        in_specs=[HELD] * len(flat) + [ANYWHERE] * len(after),
        out_specs=(HELD, HELD),
        **params(),
    )(*flat, *after)


def products_y(rows, col, after):
    flat = [a for block in rows for a in block]

    def body(*refs):
        col_ref = refs[len(flat)]
        go_ref, stay_ref = refs[len(flat) + 1 + len(after) :]
        high, _, _, _, low = here()
        away = high ^ low
        for unit in range(2):
            mine, sibling = refs[2 * unit : 2 * unit + 2]
            for z in range(4):
                lanes = slice(z * QUARTER, (z + 1) * QUARTER)
                value = sum(
                    lax.dot_general(
                        block[:, lanes],
                        col_ref[part * ROWS : (part + 1) * ROWS, :],
                        (((0,), (0,)), ((), ())),
                        preferred_element_type=jnp.float32,
                    )
                    for part, block in ((0, mine), (1, sibling))
                )

                @pl.when(away == unit)
                def _():
                    stay_ref[z] = value

                @pl.when(away != unit)
                def _():
                    go_ref[z] = encode(value)

    return pl.pallas_call(
        body,
        out_shape=(of((4, QUARTER, HALF), jnp.int16), of((4, QUARTER, HALF), jnp.float32)),
        in_specs=[HELD] * (len(flat) + 1) + [ANYWHERE] * len(after),
        out_specs=(HELD, HELD),
        **params(),
    )(*flat, col, *after)


def merge_y(stay, got, after):
    def body(stay_ref, got_ref, after_ref, go_ref, out_ref):
        _, z, core, _, _ = here()
        for k, d in enumerate((1 + 2 * core, 2)):
            go_ref[0, k] = encode(stay_ref[z ^ d] + decode(got_ref[z ^ d]))
        for k, d in enumerate((0, 3 - 2 * core)):
            out_ref[0, k] = stay_ref[z ^ d] + decode(got_ref[z ^ d])

    return pl.pallas_call(
        body,
        out_shape=(of((1, 2, QUARTER, HALF), jnp.int16), of((1, 2, QUARTER, HALF), jnp.float32)),
        in_specs=[LOOSE, LOOSE, ANYWHERE],
        out_specs=(LOOSE, LOOSE),
        **params(),
    )(stay, got, after)


def share(stay, got, after):
    def body(stay_ref, got_ref, after_ref, keep, to_c, total):
        _, _, core, _, _ = here()
        total[...] = stay_ref[0] + decode(got_ref[0])
        keep[0] = total[pl.ds(pl.multiple_of(core * 128, 128), 128), :]
        to_c[0] = encode(total[pl.ds(pl.multiple_of((1 - core) * 128, 128), 128), :])

    return pl.pallas_call(
        body,
        out_shape=(of((1, 128, HALF), jnp.float32), of((1, 128, HALF), jnp.int16)),
        in_specs=[LOOSE, LOOSE, ANYWHERE],
        out_specs=(LOOSE, LOOSE),
        scratch_shapes=[pltpu.VMEM((QUARTER, HALF), jnp.float32)],
        **params(),
    )(stay, got, after)


def second(stay, got, after):
    units = stay.shape[0]

    def body(stay_ref, got_ref, after_ref, go_ref, out_ref):
        for u in range(units):
            go_ref[u] = encode(stay_ref[u, 1] + decode(got_ref[u, 1]))
            out_ref[u] = stay_ref[u, 0] + decode(got_ref[u, 0])

    return pl.pallas_call(
        body,
        out_shape=(of((units, QUARTER, HALF), jnp.int16), of((units, QUARTER, HALF), jnp.float32)),
        in_specs=[LOOSE, LOOSE, ANYWHERE],
        out_specs=(LOOSE, LOOSE),
        **params(),
    )(stay, got, after)


def summed_z(own, other, after):
    chunks = len(own)
    arrays = []
    for stay, got, _ in own + other:
        if not any(stay is a for a in arrays):
            arrays += [stay, got]
    places = [next(i for i, a in enumerate(arrays) if a is stay) for stay, _, _ in own + other]

    def body(*refs):
        keep, to_c, to_y, to_yc, total = refs[len(arrays) + 1 :]
        high, _, core, _, low = here()
        away = high ^ low
        mine = pl.ds(pl.multiple_of(core * 128, 128), 128)
        others = pl.ds(pl.multiple_of((1 - core) * 128, 128), 128)
        for k in range(chunks):
            for side in range(2):
                n = side * chunks + k
                unit = (own + other)[n][2]
                total[k, side] = refs[places[n]][unit] + decode(refs[places[n] + 1][unit])
            to_y[k] = encode(total[k, 1 - away, mine, :])
            to_yc[k] = encode(total[k, 1 - away, others, :])
            to_c[k] = encode(total[k, away, others, :])
            keep[k] = total[k, away, mine, :]

    return pl.pallas_call(
        body,
        out_shape=(of((chunks, 128, HALF), jnp.float32),) + (of((chunks, 128, HALF), jnp.int16),) * 3,
        in_specs=[LOOSE] * len(arrays) + [ANYWHERE],
        out_specs=(LOOSE,) * 4,
        scratch_shapes=[pltpu.VMEM((chunks, 2, QUARTER, HALF), jnp.float32)],
        **params(),
    )(*arrays, after)


def finish(parts, after, out=None):
    rows = 32
    flat = [a for part in parts for a in part[1:]]

    def body(*refs):
        out_ref = refs[-1]

        def step(i, carry):
            at = pl.ds(pl.multiple_of(i * rows, rows), rows)
            if out is not None:
                held = pl.ds(pl.multiple_of(i * rows * 32, rows * 32), rows * 32)
                out_ref[held, :] = refs[len(flat)][held, :]
            first = 0
            for part in parts:
                held = refs[first : first + len(part) - 1]
                first += len(part) - 1
                for k in range(part[1].shape[0]):
                    mine, others = held[0][k, at, :], decode(held[1][k, at, :])
                    if len(held) == 4:
                        mine, others = mine + decode(held[2][k, at, :]), others + decode(held[3][k, at, :])
                    for other, value in ((False, mine), (True, others)):
                        value = value * (1.0 / CELLS)
                        base = i * (rows * 32) + out_place(part[0] + k, other)
                        for q in range(4):
                            out_ref[pl.ds(base + 4 * q, rows, stride=32), :] = value[:, q * 128 : (q + 1) * 128]
            return carry

        lax.fori_loop(0, 128 // rows, step, 0)

    operands = flat if out is None else flat + [out]
    return pl.pallas_call(
        body,
        out_shape=of((4096, 128), jnp.float32),
        in_specs=[LOOSE] * len(flat) + ([] if out is None else [HELD]) + [ANYWHERE],
        out_specs=HELD,
        input_output_aliases={} if out is None else {len(flat): 0},
        **params(),
    )(*operands, after)


def shared(stay, to_c, to_y, to_yc):
    return stay, send(to_c, TO_CORE), send(to_y, TO_YHI), send(to_yc, TO_YHI_CORE)


def per_device(counts, gene_mean, gene_scale):
    counts = counts.reshape(ROWS * 8, 128)

    part, whole = take(counts, gene_mean.reshape(8, 128), gene_scale.reshape(8, 128))
    part_y = send(part, TO_YLO)
    (whole,) = gate([whole], part)
    y_counts = send(whole, TO_YLO)
    pair = join(part, part_y, whole)
    left, opposite, right = [send(pair, to) for to in TO_X]
    first, other = halves(whole, pair)
    n0 = send(first, TO_SAME), send(other, TO_CROSS)
    total = pair[:TILES] + left[:TILES] + opposite[:TILES] + right[:TILES]
    total_sibling = send(total, TO_CORE)

    own = standardize(whole, total, part, other)
    own = own, send(own, TO_CORE)
    n1 = other_half(*own, mark(own[0]), total_sibling)
    go_0, stay_0 = products([own], [own], [n1])
    n1 = send(n1, TO_SAME)
    got_0 = send(go_0, TO_Z_FIRST)
    n0, passed = standardize_near(*n0, total, total_sibling, right, left, go_0)
    n0, x2 = (n0,), (send(passed, TO_SAME),)
    go_1, stay_1 = products([own], [n0], [go_0])
    got_1 = send(go_1, TO_Z_FIRST)
    next_0, stay_0 = second(stay_0, got_0, go_1)
    round_0 = stay_0, send(next_0, TO_Z_SECOND)
    y = standardize(y_counts, total, part_y, next_0)
    y = y, send(y, TO_CORE)
    next_1, stay_1 = second(stay_1, got_1, y[0])
    round_1 = stay_1, send(next_1, TO_Z_SECOND)
    go_2, stay_2 = products([y], [own, n0], [next_1])
    got_2 = send(go_2, TO_Z_FIRST)
    go_3, stay_3 = products_y([own, y], n1, [go_2])
    got_3 = send(go_3, TO_YHI)
    next_2, stay_2 = second(stay_2, got_2, go_3)
    round_2 = stay_2, send(next_2, TO_Z_SECOND)
    go_4, stay_4 = products([own, y], [x2], [next_2])
    got_4 = send(go_4, TO_Z_FIRST)
    sums_a = summed_z([(*round_0, 0), (*round_1, 0)], [(*round_2, 0), (*round_2, 1)], go_4)
    chunks_a = shared(*sums_a)
    go_3, stay_3 = merge_y(stay_3, got_3, sums_a[0])
    got_3 = send(go_3, TO_Z_FIRST)
    next_4, stay_4 = second(stay_4, got_4, go_3)
    round_4 = stay_4, send(next_4, TO_Z_SECOND)
    next_3, stay_3 = second(stay_3, got_3, next_4)
    got_3 = send(next_3, TO_Z_SECOND)
    out = finish([(0, *chunks_a)], next_3)
    sums_c = summed_z([(*round_4, 0)], [(*round_4, 1)], out)
    chunks_c = shared(*sums_c)
    keep_b, to_c = share(stay_3, got_3, sums_c[0])
    chunks_b = keep_b, send(to_c, TO_CORE)
    out = finish([(2, *chunks_b), (3, *chunks_c)], mark(keep_b), out)
    return out.reshape(128, 8, 4, 128).transpose(0, 2, 1, 3).reshape(1, 128, 1, 4, SPAN)


def solution(mesh):
    placed = (P("cells", "grow", "gcol", None), P("grow", "gcol", None), P("grow", "gcol", None))
    return jax.shard_map(
        per_device,
        mesh=mesh,
        in_specs=placed,
        out_specs=P("grow", "cells", "gcol", None, None),
        check_vma=False,
    )
```

```python
import jax
import jax.numpy as jnp
import numpy as np
from jax import lax
from jax.experimental import pallas as pl
from jax.experimental.pallas import tpu as pltpu
from jax.sharding import PartitionSpec as P

GENES = 8192
CELLS = 18432
AXES = ("cells", "grow", "gcol")
SIZES = (2, 4, 2, 4, 2)
ROWS = 1152
TILES = ROWS // 128
SPAN = 1024
HALF = 512
QUARTER = 256

ALPHA = 2.0**17 / 9.0e6
BETA = 32700.0 / float(np.log1p(2.0**17))
VMEM = 16 * 1024 * 1024
STREAMED = 58 * 1024 * 1024


def moves(target):
    pairs = []
    for i, at in enumerate(np.ndindex(*SIZES)):
        to = tuple(v % s for v, s in zip(target(*at), SIZES))
        pairs.append((i, int(np.ravel_multi_index(to, SIZES))))
    return pairs


TO_CORE = moves(lambda h, z, c, x, b: (h, z, 1 - c, x, b))
TO_YLO = moves(lambda h, z, c, x, b: (h, z, c, x, 1 - b))
TO_YHI = moves(lambda h, z, c, x, b: (1 - h, z, c, x, b))
TO_YHI_CORE = moves(lambda h, z, c, x, b: (1 - h, z, 1 - c, x, b))
TO_X = [moves(lambda h, z, c, x, b, d=d: (h, z, c, x + d, b)) for d in (1, 2, 3)]
FIRST = (1, 3)
TO_Z_FIRST = moves(lambda h, z, c, x, b: (h, z ^ FIRST[c], c, x, b))
TO_Z_SECOND = moves(lambda h, z, c, x, b: (h, z ^ FIRST[1 - c], c, x, b))
TO_SAME = moves(lambda h, z, c, x, b: (h, z, c, x - 1 + 2 * c, b))
TO_CROSS = moves(lambda h, z, c, x, b: (h, z, 1 - c, x + 1 - 2 * c, b))

def here():
    cells = lax.axis_index("cells")
    return cells >> 3, (cells >> 1) & 3, cells & 1, lax.axis_index("grow"), lax.axis_index("gcol")


def z_rows():
    _, z, core, _, _ = here()
    return [(z ^ d) * QUARTER for d in (0, 3 - 2 * core)], [(z ^ d) * QUARTER for d in (1 + 2 * core, 2)]


def out_place(chunk, other):
    _, _, core, x, _ = here()
    core = 1 - core if other else core
    near = (x + 1 - 2 * core) & 3
    block, half = ((x, core), (near, core), (near, 1 - core), (x ^ 2, core))[chunk]
    return half * 16 + block


def send(value, pairs):
    return lax.ppermute(value, AXES, pairs)


def encode(total):
    size = jnp.log(1.0 + ALPHA * jnp.abs(total)) * BETA + 0.5
    code = size.astype(jnp.int32)
    return jnp.where(total < 0, -code, code).astype(jnp.int16)


def decode(code):
    code = code.astype(jnp.int32).astype(jnp.float32)
    size = (jnp.exp(jnp.abs(code) * (1.0 / BETA)) - 1.0) * (1.0 / ALPHA)
    return jnp.where(code < 0, -size, size)


def params(vmem=VMEM, flops=30_000_000_000):
    return dict(
        compiler_params=pltpu.CompilerParams(vmem_limit_bytes=vmem),
        cost_estimate=pl.CostEstimate(flops=flops, bytes_accessed=1_000_000, transcendentals=0),
    )


HELD = pl.BlockSpec(memory_space=pltpu.VMEM)
LOOSE = pl.BlockSpec()
ANYWHERE = pl.BlockSpec(memory_space=pl.ANY)


def of(shape, dtype):
    return jax.ShapeDtypeStruct(shape, dtype)


def take(counts, mean, scale):
    def body(counts_ref, mean_ref, scale_ref, out_ref, narrow_ref, first_ref, other_ref, counts_v, mean_v, scale_v, sems):
        _, _, core, _, _ = here()
        parts = []
        for i in range(TILES):
            rows = pl.ds(i * 1024, 1024)
            parts.append(pltpu.make_async_copy(counts_ref.at[rows], counts_v.at[rows], sems.at[i]))
        genes = [
            pltpu.make_async_copy(mean_ref, mean_v, sems.at[TILES]),
            pltpu.make_async_copy(scale_ref, scale_v, sems.at[TILES + 1]),
        ]
        for c in parts + genes:
            c.start()
        for i in range(TILES):
            parts[i].wait()
            total = None
            at = slice(i * 128, (i + 1) * 128)
            for j in range(8):
                value = counts_v[pl.ds(i * 1024 + j, 128, stride=8), :]
                narrow_ref[at, j * 128 : (j + 1) * 128] = value.astype(jnp.int16)
                total = value if total is None else total + value
            for low, (low_ref, high_ref) in enumerate(((first_ref, other_ref), (other_ref, first_ref))):

                @pl.when(core == low)
                def _():
                    low_ref[at, :] = narrow_ref[at, 0:HALF]
                    high_ref[at, :] = narrow_ref[at, HALF:SPAN]

            out_ref[i : i + 1, :] = jnp.sum(total.astype(jnp.float32).T, axis=0, keepdims=True)
        for c in genes:
            c.wait()
        inverse = 1.0 / scale_v[...]
        out_ref[TILES : TILES + 8, :] = inverse
        out_ref[TILES + 8 : TILES + 16, :] = mean_v[...] * inverse

    return pl.pallas_call(
        body,
        out_shape=(of((TILES + 16, 128), jnp.float32), of((ROWS, SPAN), jnp.int16)) + (of((ROWS, HALF), jnp.int16),) * 2,
        in_specs=[pl.BlockSpec(memory_space=pltpu.HBM)] * 3,
        out_specs=(LOOSE, HELD, HELD, HELD),
        scratch_shapes=[
            pltpu.VMEM((ROWS * 8, 128), jnp.int32),
            pltpu.VMEM((8, 128), jnp.float32),
            pltpu.VMEM((8, 128), jnp.float32),
            pltpu.SemaphoreType.DMA((TILES + 2,)),
        ],
        **params(STREAMED),
    )(counts, mean, scale)


def gate(arrays, after):
    n = len(arrays)
    return pl.pallas_call(
        lambda *refs: None,
        out_shape=tuple(of(a.shape, a.dtype) for a in arrays),
        in_specs=[pl.BlockSpec(memory_space=pl.ANY)] * (n + 1),
        out_specs=[pl.BlockSpec(memory_space=pl.ANY)] * n,
        input_output_aliases={k: k for k in range(n)},
        **params(),
    )(*arrays, after)


def join(part, part_y, after):
    def body(part_ref, y_ref, after_ref, out_ref):
        out_ref[0:TILES, :] = part_ref[0:TILES, :] + y_ref[0:TILES, :]
        out_ref[TILES:, :] = part_ref[TILES:, :]

    return pl.pallas_call(
        body,
        out_shape=of(part.shape, part.dtype),
        in_specs=[LOOSE, LOOSE, ANYWHERE],
        out_specs=LOOSE,
        **params(),
    )(part, part_y, after)


def spread(total_refs, factor_v):
    for k in range(TILES):
        row = sum(ref[k : k + 1, :] for ref in total_refs)
        factor_v[k * 128 : (k + 1) * 128, :] = jnp.broadcast_to(GENES / row, (128, 128)).T


def standardized(count, factor, inverse, shift):
    value = count.astype(jnp.int32).astype(jnp.float32)
    return (jnp.log(1.0 + value * factor) * inverse - shift).astype(jnp.bfloat16)


def by_tiles(run):
    def step(t, carry):
        run(pl.multiple_of(t * 128, 128))
        return carry

    lax.fori_loop(0, TILES, step, 0)


def standardize(counts, total, gene, after):
    def body(counts_ref, total_ref, gene_ref, after_ref, out_ref, factor_v):
        spread([total_ref], factor_v)

        def tile(at):
            rows = pl.ds(at, 128)
            factor = factor_v[rows, :]
            for j in range(8):
                lanes = slice(j * 128, (j + 1) * 128)
                inverse, shift = gene_ref[TILES + j : TILES + j + 1, :], gene_ref[TILES + 8 + j : TILES + 9 + j, :]
                out_ref[rows, lanes] = standardized(counts_ref[rows, lanes], factor, inverse, shift)

        by_tiles(tile)

    return pl.pallas_call(
        body,
        out_shape=of((ROWS, SPAN), jnp.bfloat16),
        in_specs=[HELD, HELD, HELD, ANYWHERE],
        out_specs=HELD,
        scratch_shapes=[pltpu.VMEM((ROWS, 128), jnp.float32)],
        **params(),
    )(counts, total, gene, after)


def mark(after):
    def body(after_ref, out_ref):
        out_ref[...] = jnp.zeros((8, 128), jnp.float32)

    return pl.pallas_call(
        body, out_shape=of((8, 128), jnp.float32), in_specs=[ANYWHERE], out_specs=HELD, **params()
    )(after)


def other_half(mine, sibling, *after):
    def body(mine_ref, sibling_ref, *rest):
        out_ref = rest[-1]
        _, _, core, _, _ = here()

        def run(lanes):
            def tile(at):
                out_ref[pl.ds(at, 128), :] = mine_ref[pl.ds(at, 128), lanes]
                out_ref[pl.ds(at + ROWS, 128), :] = sibling_ref[pl.ds(at, 128), lanes]

            by_tiles(tile)

        @pl.when(core == 0)
        def _():
            run(slice(HALF, SPAN))

        @pl.when(core != 0)
        def _():
            run(slice(0, HALF))

    return pl.pallas_call(
        body,
        out_shape=of((2 * ROWS, HALF), mine.dtype),
        in_specs=[HELD, HELD] + [ANYWHERE] * len(after),
        out_specs=HELD,
        **params(),
    )(mine, sibling, *after)


def standardize_near(mine, sibling, total, total_sibling, right, left, after):
    def body(mine_ref, sibling_ref, t_ref, ts_ref, right_ref, left_ref, after_ref, out_ref, copy_ref, factor_v, gene_v):
        _, _, core, _, _ = here()
        gene_v[...] = jnp.where(core == 0, right_ref[...], left_ref[...])
        for part, count_ref, total_ref in ((0, mine_ref, t_ref), (1, sibling_ref, ts_ref)):
            spread([total_ref], factor_v)

            def tile(at, part=part, count_ref=count_ref):
                factor = factor_v[pl.ds(at, 128), :]
                for j in range(4):
                    lanes = slice(j * 128, (j + 1) * 128)
                    g = TILES + core * 4 + j
                    inverse, shift = gene_v[pl.ds(g, 1), :], gene_v[pl.ds(g + 8, 1), :]
                    value = standardized(count_ref[pl.ds(at, 128), lanes], factor, inverse, shift)
                    out_ref[pl.ds(at + part * ROWS, 128), lanes] = value
                    copy_ref[pl.ds(at + part * ROWS, 128), lanes] = value

            by_tiles(tile)

    return pl.pallas_call(
        body,
        out_shape=(of((2 * ROWS, HALF), jnp.bfloat16),) * 2,
        in_specs=[HELD] * 6 + [ANYWHERE],
        out_specs=(HELD, HELD),
        scratch_shapes=[pltpu.VMEM((ROWS, 128), jnp.float32), pltpu.VMEM((TILES + 16, 128), jnp.float32)],
        **params(),
    )(mine, sibling, total, total_sibling, right, left, after)


def products(rows, cols, after, far=False):
    n_rows, n_cols = len(rows), len(cols)
    units = max(n_rows, n_cols)
    flat = [a for block in rows + cols for a in block]

    def body(*refs):
        go_ref, stay_ref, *scratch = refs[len(flat) + len(after) :]
        _, _, core, _, _ = here()
        stays, goes = z_rows()
        blocks, k = [], 0
        for block in rows + cols:
            blocks.append(refs[k : k + len(block)])
            k += len(block)

        copies = []
        if far:
            col_v, sems = scratch
            for part in range(2):
                half = pl.ds(part * ROWS, ROWS)
                copies.append(pltpu.make_async_copy(blocks[-1][0].at[half], col_v.at[half], sems.at[part]))
                copies[part].start()
            blocks[-1] = (col_v,)

        def right(col, part):
            if len(col) == 1:
                return col[0][part * ROWS : (part + 1) * ROWS, :]
            if col[part].shape[1] == SPAN:
                return col[part][:, pl.ds(pl.multiple_of(core * HALF, HALF), HALF)]
            return col[part][...]

        for unit in range(units):
            row = blocks[unit if n_rows > 1 else 0]
            col = blocks[n_rows + (unit if n_cols > 1 else 0)]

            def product(at):
                at = pl.multiple_of(at, QUARTER)
                terms = []
                for part in range(2):
                    if copies:
                        copies.pop(0).wait()
                    terms.append(
                        lax.dot_general(
                            row[part][:, pl.ds(at, QUARTER)],
                            right(col, part),
                            (((0,), (0,)), ((), ())),
                            preferred_element_type=jnp.float32,
                        )
                    )
                return terms[0] + terms[1]

            for k in range(2):
                go_ref[unit, k] = encode(product(goes[k]))
            for k in range(2):
                stay_ref[unit, k] = product(stays[k])

    return pl.pallas_call(
        body,
        out_shape=(of((units, 2, QUARTER, HALF), jnp.int16), of((units, 2, QUARTER, HALF), jnp.float32)),
        in_specs=[HELD] * (len(flat) - far) + [pl.BlockSpec(memory_space=pltpu.HBM)] * far + [ANYWHERE] * len(after),
        out_specs=(HELD, HELD),
        scratch_shapes=[pltpu.VMEM((2 * ROWS, HALF), jnp.bfloat16), pltpu.SemaphoreType.DMA((2,))] if far else [],
        **params(flops=12_000_000_000),
    )(*flat, *after)


def products_y(rows, col, after):
    flat = [a for block in rows for a in block]

    def body(*refs):
        col_ref = refs[len(flat)]
        go_ref, stay_ref, col_v, sems = refs[len(flat) + 1 + len(after) :]
        copies = []
        for part in range(2):
            half = pl.ds(part * ROWS, ROWS)
            copies.append(pltpu.make_async_copy(col_ref.at[half], col_v.at[half], sems.at[part]))
            copies[part].start()
        high, _, _, _, low = here()
        away = high ^ low
        def run(units):
            waits = list(copies)
            for unit, goes in units:
                mine, sibling = refs[2 * unit : 2 * unit + 2]
                for z in range(4):
                    lanes = slice(z * QUARTER, (z + 1) * QUARTER)
                    terms = []
                    for part, block in ((0, mine), (1, sibling)):
                        if waits:
                            waits.pop(0).wait()
                        terms.append(
                            lax.dot_general(
                                block[:, lanes],
                                col_v[part * ROWS : (part + 1) * ROWS, :],
                                (((0,), (0,)), ((), ())),
                                preferred_element_type=jnp.float32,
                            )
                        )
                    if goes:
                        go_ref[z] = encode(terms[0] + terms[1])
                    else:
                        stay_ref[z] = terms[0] + terms[1]

        @pl.when(away == 0)
        def _():
            run(((1, True), (0, False)))

        @pl.when(away != 0)
        def _():
            run(((0, True), (1, False)))

    return pl.pallas_call(
        body,
        out_shape=(of((4, QUARTER, HALF), jnp.int16), of((4, QUARTER, HALF), jnp.float32)),
        in_specs=[HELD] * len(flat) + [pl.BlockSpec(memory_space=pltpu.HBM)] + [ANYWHERE] * len(after),
        out_specs=(HELD, HELD),
        scratch_shapes=[pltpu.VMEM((2 * ROWS, HALF), jnp.bfloat16), pltpu.SemaphoreType.DMA((2,))],
        **params(flops=12_000_000_000),
    )(*flat, col, *after)


def merge_y(stay, got, after):
    def body(stay_ref, got_ref, after_ref, go_ref, out_ref):
        _, z, core, _, _ = here()
        for k, d in enumerate((1 + 2 * core, 2)):
            go_ref[0, k] = encode(stay_ref[z ^ d] + decode(got_ref[z ^ d]))
        for k, d in enumerate((0, 3 - 2 * core)):
            out_ref[0, k] = stay_ref[z ^ d] + decode(got_ref[z ^ d])

    return pl.pallas_call(
        body,
        out_shape=(of((1, 2, QUARTER, HALF), jnp.int16), of((1, 2, QUARTER, HALF), jnp.float32)),
        in_specs=[LOOSE, LOOSE, ANYWHERE],
        out_specs=(LOOSE, LOOSE),
        **params(),
    )(stay, got, after)


def share(stay, got, after):
    def body(stay_ref, got_ref, after_ref, keep, to_c, total):
        _, _, core, _, _ = here()
        total[...] = stay_ref[0] + decode(got_ref[0])
        keep[0] = total[pl.ds(pl.multiple_of(core * 128, 128), 128), :]
        to_c[0] = encode(total[pl.ds(pl.multiple_of((1 - core) * 128, 128), 128), :])

    return pl.pallas_call(
        body,
        out_shape=(of((1, 128, HALF), jnp.float32), of((1, 128, HALF), jnp.int16)),
        in_specs=[LOOSE, LOOSE, ANYWHERE],
        out_specs=(LOOSE, LOOSE),
        scratch_shapes=[pltpu.VMEM((QUARTER, HALF), jnp.float32)],
        **params(),
    )(stay, got, after)


def second(stay, got, after):
    units = stay.shape[0]

    def body(stay_ref, got_ref, after_ref, go_ref, out_ref):
        for u in range(units):
            go_ref[u] = encode(stay_ref[u, 1] + decode(got_ref[u, 1]))
            out_ref[u] = stay_ref[u, 0] + decode(got_ref[u, 0])

    return pl.pallas_call(
        body,
        out_shape=(of((units, QUARTER, HALF), jnp.int16), of((units, QUARTER, HALF), jnp.float32)),
        in_specs=[LOOSE, LOOSE, ANYWHERE],
        out_specs=(LOOSE, LOOSE),
        **params(),
    )(stay, got, after)


def summed_z(own, other, after):
    chunks = len(own)
    arrays = []
    for stay, got, _ in own + other:
        if not any(stay is a for a in arrays):
            arrays += [stay, got]
    places = [next(i for i, a in enumerate(arrays) if a is stay) for stay, _, _ in own + other]

    def body(*refs):
        keep, to_c, to_y, to_yc, total = refs[len(arrays) + 1 :]
        high, _, core, _, low = here()
        away = high ^ low
        mine = pl.ds(pl.multiple_of(core * 128, 128), 128)
        others = pl.ds(pl.multiple_of((1 - core) * 128, 128), 128)
        for k in range(chunks):
            for side in range(2):
                n = side * chunks + k
                unit = (own + other)[n][2]
                total[k, side] = refs[places[n]][unit] + decode(refs[places[n] + 1][unit])
            to_y[k] = encode(total[k, 1 - away, mine, :])
            to_yc[k] = encode(total[k, 1 - away, others, :])
            to_c[k] = encode(total[k, away, others, :])
            keep[k] = total[k, away, mine, :]

    return pl.pallas_call(
        body,
        out_shape=(of((chunks, 128, HALF), jnp.float32),) + (of((chunks, 128, HALF), jnp.int16),) * 3,
        in_specs=[LOOSE] * len(arrays) + [ANYWHERE],
        out_specs=(LOOSE,) * 4,
        scratch_shapes=[pltpu.VMEM((chunks, 2, QUARTER, HALF), jnp.float32)],
        **params(),
    )(*arrays, after)


def presum(keep, got_c, got_y, got_yc, after):
    def body(keep_ref, c_ref, y_ref, yc_ref, after_ref, mine_ref, others_ref):
        for k in range(keep.shape[0]):
            mine_ref[k] = keep_ref[k] + decode(y_ref[k])
            others_ref[k] = decode(c_ref[k]) + decode(yc_ref[k])

    return pl.pallas_call(
        body,
        out_shape=(of(keep.shape, jnp.float32),) * 2,
        in_specs=[LOOSE] * 4 + [ANYWHERE],
        out_specs=(LOOSE, LOOSE),
        **params(),
    )(keep, got_c, got_y, got_yc, after)


def finish(done, chunk_2, chunk_3, after):
    rows = 32

    def body(mine_ref, others_ref, keep_2, c_2, keep_3, c_3, y_3, yc_3, after_ref, out_ref):
        def put(chunk, mine, others):
            for other, value in ((False, mine), (True, others)):
                value = value * (1.0 / CELLS)
                base = out_place(chunk, other)
                for q in range(4):
                    out_ref[pl.ds(base + 4 * q, rows, stride=32), :] = value[:, q * 128 : (q + 1) * 128]

        for k in range(2):
            put(k, mine_ref[k], others_ref[k])
        put(2, keep_2[0], decode(c_2[0]))
        put(3, keep_3[0] + decode(y_3[0]), decode(c_3[0]) + decode(yc_3[0]))

    def block(n):
        return pl.BlockSpec((n, rows, HALF), lambda i: (0, i, 0))

    return pl.pallas_call(
        body,
        out_shape=of((4096, 128), jnp.float32),
        grid=(128 // rows,),
        in_specs=[block(2)] * 2 + [block(1)] * 6 + [ANYWHERE],
        out_specs=pl.BlockSpec((rows * 32, 128), lambda i: (i, 0)),
        **params(),
    )(*done, *chunk_2, *chunk_3, after)


def shared(stay, to_c, to_y, to_yc):
    return stay, send(to_c, TO_CORE), send(to_y, TO_YHI), send(to_yc, TO_YHI_CORE)


def per_device(counts, gene_mean, gene_scale):
    counts = counts.reshape(ROWS * 8, 128)

    part, whole, first, other = take(counts, gene_mean.reshape(8, 128), gene_scale.reshape(8, 128))
    part_y = send(part, TO_YLO)
    (whole,) = gate([whole], part)
    y_counts = send(whole, TO_YLO)
    pair = join(part, part_y, whole)
    left, opposite, right = [send(pair, to) for to in TO_X]
    first, other = gate([first, other], pair)
    n0 = send(first, TO_SAME), send(other, TO_CROSS)
    total = pair[:TILES] + left[:TILES] + opposite[:TILES] + right[:TILES]
    total_sibling = send(total, TO_CORE)

    own = standardize(whole, total, part, other)
    own = own, send(own, TO_CORE)
    n1 = other_half(*own, mark(own[0]), total_sibling)
    go_0, stay_0 = products([own], [own], [n1])
    n1 = send(n1, TO_SAME)
    got_0 = send(go_0, TO_Z_FIRST)
    n0, passed = standardize_near(*n0, total, total_sibling, right, left, go_0)
    n0, x2 = (n0,), (send(passed, TO_SAME),)
    go_1, stay_1 = products([own], [n0], [go_0])
    got_1 = send(go_1, TO_Z_FIRST)
    next_0, stay_0 = second(stay_0, got_0, go_1)
    round_0 = stay_0, send(next_0, TO_Z_SECOND)
    y = standardize(y_counts, total, part_y, next_0)
    y = y, send(y, TO_CORE)
    next_1, stay_1 = second(stay_1, got_1, y[0])
    round_1 = stay_1, send(next_1, TO_Z_SECOND)
    go_2, stay_2 = products([y], [own, n0], [next_1])
    got_2 = send(go_2, TO_Z_FIRST)
    go_3, stay_3 = products_y([own, y], n1, [go_2, round_0[1], round_1[1]])
    got_3 = send(go_3, TO_YHI)
    next_2, stay_2 = second(stay_2, got_2, go_3)
    round_2 = stay_2, send(next_2, TO_Z_SECOND)
    go_4, stay_4 = products([own, y], [x2], [next_2])
    got_4 = send(go_4, TO_Z_FIRST)
    sums_a = summed_z([(*round_0, 0), (*round_1, 0)], [(*round_2, 0), (*round_2, 1)], go_4)
    chunks_a = shared(*sums_a)
    go_3, stay_3 = merge_y(stay_3, got_3, sums_a[0])
    got_3 = send(go_3, TO_Z_FIRST)
    next_4, stay_4 = second(stay_4, got_4, go_3)
    round_4 = stay_4, send(next_4, TO_Z_SECOND)
    next_3, stay_3 = second(stay_3, got_3, next_4)
    got_3 = send(next_3, TO_Z_SECOND)
    done_a = presum(*chunks_a, next_3)
    sums_c = summed_z([(*round_4, 0)], [(*round_4, 1)], done_a[0])
    chunks_c = shared(*sums_c)
    keep_b, to_c = share(stay_3, got_3, sums_c[0])
    out = finish(done_a, (keep_b, send(to_c, TO_CORE)), chunks_c, mark(keep_b))
    return out.reshape(128, 8, 4, 128).transpose(0, 2, 1, 3).reshape(1, 128, 1, 4, SPAN)


def solution(mesh):
    placed = (P("cells", "grow", "gcol", None), P("grow", "gcol", None), P("grow", "gcol", None))
    return jax.shard_map(
        per_device,
        mesh=mesh,
        in_specs=placed,
        out_specs=P("grow", "cells", "gcol", None, None),
        check_vma=False,
    )
```

```python
import jax
import jax.numpy as jnp
import numpy as np
from jax import lax
from jax.experimental import pallas as pl
from jax.experimental.pallas import tpu as pltpu
from jax.sharding import PartitionSpec as P

GENES = 8192
CELLS = 18432
AXES = ("cells", "grow", "gcol")
SIZES = (2, 4, 2, 4, 2)
ROWS = 1152
TILES = ROWS // 128
SPAN = 1024
HALF = 512
QUARTER = 256

ALPHA = 2.0**17 / 9.0e6
BETA = 32700.0 / float(np.log1p(2.0**17))
VMEM = 16 * 1024 * 1024
STREAMED = 58 * 1024 * 1024


def moves(target):
    pairs = []
    for i, at in enumerate(np.ndindex(*SIZES)):
        to = tuple(v % s for v, s in zip(target(*at), SIZES))
        pairs.append((i, int(np.ravel_multi_index(to, SIZES))))
    return pairs


TO_CORE = moves(lambda h, z, c, x, b: (h, z, 1 - c, x, b))
TO_YLO = moves(lambda h, z, c, x, b: (h, z, c, x, 1 - b))
TO_YHI = moves(lambda h, z, c, x, b: (1 - h, z, c, x, b))
TO_YHI_CORE = moves(lambda h, z, c, x, b: (1 - h, z, 1 - c, x, b))
TO_X = [moves(lambda h, z, c, x, b, d=d: (h, z, c, x + d, b)) for d in (1, 2, 3)]
FIRST = (1, 3)
TO_Z_FIRST = moves(lambda h, z, c, x, b: (h, z ^ FIRST[c], c, x, b))
TO_Z_SECOND = moves(lambda h, z, c, x, b: (h, z ^ FIRST[1 - c], c, x, b))
TO_SAME = moves(lambda h, z, c, x, b: (h, z, c, x - 1 + 2 * c, b))
TO_CROSS = moves(lambda h, z, c, x, b: (h, z, 1 - c, x + 1 - 2 * c, b))

def here():
    cells = lax.axis_index("cells")
    return cells >> 3, (cells >> 1) & 3, cells & 1, lax.axis_index("grow"), lax.axis_index("gcol")


def z_rows():
    _, z, core, _, _ = here()
    return [(z ^ d) * QUARTER for d in (0, 3 - 2 * core)], [(z ^ d) * QUARTER for d in (1 + 2 * core, 2)]


def out_place(chunk, other):
    _, _, core, x, _ = here()
    core = 1 - core if other else core
    near = (x + 1 - 2 * core) & 3
    block, half = ((x, core), (near, core), (near, 1 - core), (x ^ 2, core))[chunk]
    return half * 16 + block


def send(value, pairs):
    return lax.ppermute(value, AXES, pairs)


def encode(total):
    size = jnp.log(1.0 + ALPHA * jnp.abs(total)) * BETA + 0.5
    code = size.astype(jnp.int32)
    return jnp.where(total < 0, -code, code).astype(jnp.int16)


def decode(code):
    code = code.astype(jnp.int32).astype(jnp.float32)
    size = (jnp.exp(jnp.abs(code) * (1.0 / BETA)) - 1.0) * (1.0 / ALPHA)
    return jnp.where(code < 0, -size, size)


def params(vmem=VMEM, flops=30_000_000_000):
    return dict(
        compiler_params=pltpu.CompilerParams(vmem_limit_bytes=vmem),
        cost_estimate=pl.CostEstimate(flops=flops, bytes_accessed=1_000_000, transcendentals=0),
    )


HELD = pl.BlockSpec(memory_space=pltpu.VMEM)
LOOSE = pl.BlockSpec()
ANYWHERE = pl.BlockSpec(memory_space=pl.ANY)


def of(shape, dtype):
    return jax.ShapeDtypeStruct(shape, dtype)


def take(counts, mean, scale):
    def body(counts_ref, mean_ref, scale_ref, out_ref, narrow_ref, first_ref, other_ref, counts_v, mean_v, scale_v, sems):
        _, _, core, _, _ = here()
        parts = []
        for i in range(TILES):
            rows = pl.ds(i * 1024, 1024)
            parts.append(pltpu.make_async_copy(counts_ref.at[rows], counts_v.at[rows], sems.at[i]))
        genes = [
            pltpu.make_async_copy(mean_ref, mean_v, sems.at[TILES]),
            pltpu.make_async_copy(scale_ref, scale_v, sems.at[TILES + 1]),
        ]
        for c in parts + genes:
            c.start()
        for i in range(TILES):
            parts[i].wait()
            total = None
            at = slice(i * 128, (i + 1) * 128)
            for j in range(8):
                value = counts_v[pl.ds(i * 1024 + j, 128, stride=8), :]
                narrow_ref[at, j * 128 : (j + 1) * 128] = value.astype(jnp.int16)
                total = value if total is None else total + value
            for low, (low_ref, high_ref) in enumerate(((first_ref, other_ref), (other_ref, first_ref))):

                @pl.when(core == low)
                def _():
                    low_ref[at, :] = narrow_ref[at, 0:HALF]
                    high_ref[at, :] = narrow_ref[at, HALF:SPAN]

            out_ref[i : i + 1, :] = jnp.sum(total.astype(jnp.float32).T, axis=0, keepdims=True)
        for c in genes:
            c.wait()
        inverse = 1.0 / scale_v[...]
        out_ref[TILES : TILES + 8, :] = inverse
        out_ref[TILES + 8 : TILES + 16, :] = mean_v[...] * inverse

    return pl.pallas_call(
        body,
        out_shape=(of((TILES + 16, 128), jnp.float32), of((ROWS, SPAN), jnp.int16)) + (of((ROWS, HALF), jnp.int16),) * 2,
        in_specs=[pl.BlockSpec(memory_space=pltpu.HBM)] * 3,
        out_specs=(LOOSE, HELD, HELD, HELD),
        scratch_shapes=[
            pltpu.VMEM((ROWS * 8, 128), jnp.int32),
            pltpu.VMEM((8, 128), jnp.float32),
            pltpu.VMEM((8, 128), jnp.float32),
            pltpu.SemaphoreType.DMA((TILES + 2,)),
        ],
        **params(STREAMED),
    )(counts, mean, scale)


def gate(arrays, after):
    n = len(arrays)
    return pl.pallas_call(
        lambda *refs: None,
        out_shape=tuple(of(a.shape, a.dtype) for a in arrays),
        in_specs=[pl.BlockSpec(memory_space=pl.ANY)] * (n + 1),
        out_specs=[pl.BlockSpec(memory_space=pl.ANY)] * n,
        input_output_aliases={k: k for k in range(n)},
        **params(),
    )(*arrays, after)


def join(part, part_y, after):
    def body(part_ref, y_ref, after_ref, out_ref):
        out_ref[0:TILES, :] = part_ref[0:TILES, :] + y_ref[0:TILES, :]
        out_ref[TILES:, :] = part_ref[TILES:, :]

    return pl.pallas_call(
        body,
        out_shape=of(part.shape, part.dtype),
        in_specs=[LOOSE, LOOSE, ANYWHERE],
        out_specs=LOOSE,
        **params(),
    )(part, part_y, after)


def spread(total_refs, factor_v):
    for k in range(TILES):
        row = sum(ref[k : k + 1, :] for ref in total_refs)
        factor_v[k * 128 : (k + 1) * 128, :] = jnp.broadcast_to(GENES / row, (128, 128)).T


def standardized(count, factor, inverse, shift):
    value = count.astype(jnp.int32).astype(jnp.float32)
    return (jnp.log(1.0 + value * factor) * inverse - shift).astype(jnp.bfloat16)


def by_tiles(run):
    def step(t, carry):
        run(pl.multiple_of(t * 128, 128))
        return carry

    lax.fori_loop(0, TILES, step, 0)


def standardize(counts, total, gene, after):
    def body(counts_ref, total_ref, gene_ref, after_ref, out_ref, factor_v):
        spread([total_ref], factor_v)

        def tile(at):
            rows = pl.ds(at, 128)
            factor = factor_v[rows, :]
            for j in range(8):
                lanes = slice(j * 128, (j + 1) * 128)
                inverse, shift = gene_ref[TILES + j : TILES + j + 1, :], gene_ref[TILES + 8 + j : TILES + 9 + j, :]
                out_ref[rows, lanes] = standardized(counts_ref[rows, lanes], factor, inverse, shift)

        by_tiles(tile)

    return pl.pallas_call(
        body,
        out_shape=of((ROWS, SPAN), jnp.bfloat16),
        in_specs=[HELD, HELD, HELD, ANYWHERE],
        out_specs=HELD,
        scratch_shapes=[pltpu.VMEM((ROWS, 128), jnp.float32)],
        **params(),
    )(counts, total, gene, after)


def mark(after):
    def body(after_ref, out_ref):
        out_ref[...] = jnp.zeros((8, 128), jnp.float32)

    return pl.pallas_call(
        body, out_shape=of((8, 128), jnp.float32), in_specs=[ANYWHERE], out_specs=HELD, **params()
    )(after)


def other_half(mine, sibling, *after):
    def body(mine_ref, sibling_ref, *rest):
        out_ref = rest[-1]
        _, _, core, _, _ = here()

        def run(lanes):
            def tile(at):
                out_ref[pl.ds(at, 128), :] = mine_ref[pl.ds(at, 128), lanes]
                out_ref[pl.ds(at + ROWS, 128), :] = sibling_ref[pl.ds(at, 128), lanes]

            by_tiles(tile)

        @pl.when(core == 0)
        def _():
            run(slice(HALF, SPAN))

        @pl.when(core != 0)
        def _():
            run(slice(0, HALF))

    return pl.pallas_call(
        body,
        out_shape=of((2 * ROWS, HALF), mine.dtype),
        in_specs=[HELD, HELD] + [ANYWHERE] * len(after),
        out_specs=HELD,
        **params(),
    )(mine, sibling, *after)


def standardize_near(mine, sibling, total, total_sibling, right, left, after):
    def body(mine_ref, sibling_ref, t_ref, ts_ref, right_ref, left_ref, after_ref, out_ref, copy_ref, factor_v, gene_v):
        _, _, core, _, _ = here()
        gene_v[...] = jnp.where(core == 0, right_ref[...], left_ref[...])
        for part, count_ref, total_ref in ((0, mine_ref, t_ref), (1, sibling_ref, ts_ref)):
            spread([total_ref], factor_v)

            def tile(at, part=part, count_ref=count_ref):
                factor = factor_v[pl.ds(at, 128), :]
                for j in range(4):
                    lanes = slice(j * 128, (j + 1) * 128)
                    g = TILES + core * 4 + j
                    inverse, shift = gene_v[pl.ds(g, 1), :], gene_v[pl.ds(g + 8, 1), :]
                    value = standardized(count_ref[pl.ds(at, 128), lanes], factor, inverse, shift)
                    out_ref[pl.ds(at + part * ROWS, 128), lanes] = value
                    copy_ref[pl.ds(at + part * ROWS, 128), lanes] = value

            by_tiles(tile)

    return pl.pallas_call(
        body,
        out_shape=(of((2 * ROWS, HALF), jnp.bfloat16),) * 2,
        in_specs=[HELD] * 6 + [ANYWHERE],
        out_specs=(HELD, HELD),
        scratch_shapes=[pltpu.VMEM((ROWS, 128), jnp.float32), pltpu.VMEM((TILES + 16, 128), jnp.float32)],
        **params(),
    )(mine, sibling, total, total_sibling, right, left, after)


def products(rows, cols, after, far=False):
    n_rows, n_cols = len(rows), len(cols)
    units = max(n_rows, n_cols)
    flat = [a for block in rows + cols for a in block]

    def body(*refs):
        go_ref, stay_ref, *scratch = refs[len(flat) + len(after) :]
        _, _, core, _, _ = here()
        stays, goes = z_rows()
        blocks, k = [], 0
        for block in rows + cols:
            blocks.append(refs[k : k + len(block)])
            k += len(block)

        copies = []
        if far:
            col_v, sems = scratch
            for part in range(2):
                half = pl.ds(part * ROWS, ROWS)
                copies.append(pltpu.make_async_copy(blocks[-1][0].at[half], col_v.at[half], sems.at[part]))
                copies[part].start()
            blocks[-1] = (col_v,)

        def right(col, part):
            if len(col) == 1:
                return col[0][part * ROWS : (part + 1) * ROWS, :]
            if col[part].shape[1] == SPAN:
                return col[part][:, pl.ds(pl.multiple_of(core * HALF, HALF), HALF)]
            return col[part][...]

        for unit in range(units):
            row = blocks[unit if n_rows > 1 else 0]
            col = blocks[n_rows + (unit if n_cols > 1 else 0)]

            def product(at):
                at = pl.multiple_of(at, QUARTER)
                terms = []
                for part in range(2):
                    if copies:
                        copies.pop(0).wait()
                    terms.append(
                        lax.dot_general(
                            row[part][:, pl.ds(at, QUARTER)],
                            right(col, part),
                            (((0,), (0,)), ((), ())),
                            preferred_element_type=jnp.float32,
                        )
                    )
                return terms[0] + terms[1]

            for k in range(2):
                go_ref[unit, k] = encode(product(goes[k]))
            for k in range(2):
                stay_ref[unit, k] = product(stays[k])

    return pl.pallas_call(
        body,
        out_shape=(of((units, 2, QUARTER, HALF), jnp.int16), of((units, 2, QUARTER, HALF), jnp.float32)),
        in_specs=[HELD] * (len(flat) - far) + [pl.BlockSpec(memory_space=pltpu.HBM)] * far + [ANYWHERE] * len(after),
        out_specs=(HELD, HELD),
        scratch_shapes=[pltpu.VMEM((2 * ROWS, HALF), jnp.bfloat16), pltpu.SemaphoreType.DMA((2,))] if far else [],
        **params(flops=12_000_000_000),
    )(*flat, *after)


def products_y(rows, col, after):
    flat = [a for block in rows for a in block]

    def body(*refs):
        col_ref = refs[len(flat)]
        go_ref, stay_ref, col_v, sems = refs[len(flat) + 1 + len(after) :]
        copies = []
        for part in range(2):
            half = pl.ds(part * ROWS, ROWS)
            copies.append(pltpu.make_async_copy(col_ref.at[half], col_v.at[half], sems.at[part]))
            copies[part].start()
        high, _, _, _, low = here()
        away = high ^ low
        def run(units):
            waits = list(copies)
            for unit, goes in units:
                mine, sibling = refs[2 * unit : 2 * unit + 2]
                for z in range(4):
                    lanes = slice(z * QUARTER, (z + 1) * QUARTER)
                    terms = []
                    for part, block in ((0, mine), (1, sibling)):
                        if waits:
                            waits.pop(0).wait()
                        terms.append(
                            lax.dot_general(
                                block[:, lanes],
                                col_v[part * ROWS : (part + 1) * ROWS, :],
                                (((0,), (0,)), ((), ())),
                                preferred_element_type=jnp.float32,
                            )
                        )
                    if goes:
                        go_ref[z] = encode(terms[0] + terms[1])
                    else:
                        stay_ref[z] = terms[0] + terms[1]

        @pl.when(away == 0)
        def _():
            run(((1, True), (0, False)))

        @pl.when(away != 0)
        def _():
            run(((0, True), (1, False)))

    return pl.pallas_call(
        body,
        out_shape=(of((4, QUARTER, HALF), jnp.int16), of((4, QUARTER, HALF), jnp.float32)),
        in_specs=[HELD] * len(flat) + [pl.BlockSpec(memory_space=pltpu.HBM)] + [ANYWHERE] * len(after),
        out_specs=(HELD, HELD),
        scratch_shapes=[pltpu.VMEM((2 * ROWS, HALF), jnp.bfloat16), pltpu.SemaphoreType.DMA((2,))],
        **params(flops=12_000_000_000),
    )(*flat, col, *after)


def merge_y(stay, got, *after):
    def body(stay_ref, got_ref, *rest):
        go_ref, out_ref = rest[-2:]
        _, z, core, _, _ = here()
        for k, d in enumerate((1 + 2 * core, 2)):
            go_ref[0, k] = encode(stay_ref[z ^ d] + decode(got_ref[z ^ d]))
        for k, d in enumerate((0, 3 - 2 * core)):
            out_ref[0, k] = stay_ref[z ^ d] + decode(got_ref[z ^ d])

    return pl.pallas_call(
        body,
        out_shape=(of((1, 2, QUARTER, HALF), jnp.int16), of((1, 2, QUARTER, HALF), jnp.float32)),
        in_specs=[LOOSE, LOOSE] + [ANYWHERE] * len(after),
        out_specs=(LOOSE, LOOSE),
        **params(),
    )(stay, got, *after)


def share(stay, got, *after):
    def body(stay_ref, got_ref, *rest):
        keep, to_c, total = rest[-3:]
        _, _, core, _, _ = here()
        total[...] = stay_ref[0] + decode(got_ref[0])
        keep[0] = total[pl.ds(pl.multiple_of(core * 128, 128), 128), :]
        to_c[0] = encode(total[pl.ds(pl.multiple_of((1 - core) * 128, 128), 128), :])

    return pl.pallas_call(
        body,
        out_shape=(of((1, 128, HALF), jnp.float32), of((1, 128, HALF), jnp.int16)),
        in_specs=[LOOSE, LOOSE] + [ANYWHERE] * len(after),
        out_specs=(LOOSE, LOOSE),
        scratch_shapes=[pltpu.VMEM((QUARTER, HALF), jnp.float32)],
        **params(),
    )(stay, got, *after)


def second(stay, got, after):
    units = stay.shape[0]

    def body(stay_ref, got_ref, after_ref, go_ref, out_ref):
        for u in range(units):
            go_ref[u] = encode(stay_ref[u, 1] + decode(got_ref[u, 1]))
            out_ref[u] = stay_ref[u, 0] + decode(got_ref[u, 0])

    return pl.pallas_call(
        body,
        out_shape=(of((units, QUARTER, HALF), jnp.int16), of((units, QUARTER, HALF), jnp.float32)),
        in_specs=[LOOSE, LOOSE, ANYWHERE],
        out_specs=(LOOSE, LOOSE),
        **params(),
    )(stay, got, after)


def summed_z(own, other, after):
    chunks = len(own)
    arrays = []
    for stay, got, _ in own + other:
        if not any(stay is a for a in arrays):
            arrays += [stay, got]
    places = [next(i for i, a in enumerate(arrays) if a is stay) for stay, _, _ in own + other]

    def body(*refs):
        keep, to_c, to_y, to_yc, total = refs[len(arrays) + 1 :]
        high, _, core, _, low = here()
        away = high ^ low
        mine = pl.ds(pl.multiple_of(core * 128, 128), 128)
        others = pl.ds(pl.multiple_of((1 - core) * 128, 128), 128)
        for k in range(chunks):
            for side in range(2):
                n = side * chunks + k
                unit = (own + other)[n][2]
                total[k, side] = refs[places[n]][unit] + decode(refs[places[n] + 1][unit])
            to_y[k] = encode(total[k, 1 - away, mine, :])
            to_yc[k] = encode(total[k, 1 - away, others, :])
            to_c[k] = encode(total[k, away, others, :])
            keep[k] = total[k, away, mine, :]

    return pl.pallas_call(
        body,
        out_shape=(of((chunks, 128, HALF), jnp.float32),) + (of((chunks, 128, HALF), jnp.int16),) * 3,
        in_specs=[LOOSE] * len(arrays) + [ANYWHERE],
        out_specs=(LOOSE,) * 4,
        scratch_shapes=[pltpu.VMEM((chunks, 2, QUARTER, HALF), jnp.float32)],
        **params(),
    )(*arrays, after)


def presum(keep, got_c, got_y, got_yc, after):
    def body(keep_ref, c_ref, y_ref, yc_ref, after_ref, mine_ref, others_ref):
        for k in range(keep.shape[0]):
            mine_ref[k] = keep_ref[k] + decode(y_ref[k])
            others_ref[k] = decode(c_ref[k]) + decode(yc_ref[k])

    return pl.pallas_call(
        body,
        out_shape=(of(keep.shape, jnp.float32),) * 2,
        in_specs=[LOOSE] * 4 + [ANYWHERE],
        out_specs=(LOOSE, LOOSE),
        **params(),
    )(keep, got_c, got_y, got_yc, after)


def finish(done, chunk_2, chunk_3, after):
    rows = 32

    def body(mine_ref, others_ref, keep_2, c_2, keep_3, c_3, y_3, yc_3, after_ref, out_ref):
        def put(chunk, mine, others):
            for other, value in ((False, mine), (True, others)):
                value = value * (1.0 / CELLS)
                base = out_place(chunk, other)
                for q in range(4):
                    out_ref[pl.ds(base + 4 * q, rows, stride=32), :] = value[:, q * 128 : (q + 1) * 128]

        for k in range(2):
            put(k, mine_ref[k], others_ref[k])
        put(2, keep_2[0], decode(c_2[0]))
        put(3, keep_3[0] + decode(y_3[0]), decode(c_3[0]) + decode(yc_3[0]))

    def block(n):
        return pl.BlockSpec((n, rows, HALF), lambda i: (0, i, 0))

    return pl.pallas_call(
        body,
        out_shape=of((4096, 128), jnp.float32),
        grid=(128 // rows,),
        in_specs=[block(2)] * 2 + [block(1)] * 6 + [ANYWHERE],
        out_specs=pl.BlockSpec((rows * 32, 128), lambda i: (i, 0)),
        **params(),
    )(*done, *chunk_2, *chunk_3, after)


def shared(stay, to_c, to_y, to_yc):
    return stay, send(to_c, TO_CORE), send(to_y, TO_YHI), send(to_yc, TO_YHI_CORE)


def per_device(counts, gene_mean, gene_scale):
    counts = counts.reshape(ROWS * 8, 128)

    part, whole, first, other = take(counts, gene_mean.reshape(8, 128), gene_scale.reshape(8, 128))
    part_y = send(part, TO_YLO)
    (whole,) = gate([whole], part)
    y_counts = send(whole, TO_YLO)
    pair = join(part, part_y, whole)
    left, opposite, right = [send(pair, to) for to in TO_X]
    first, other = gate([first, other], pair)
    n0 = send(first, TO_SAME), send(other, TO_CROSS)
    total = pair[:TILES] + left[:TILES] + opposite[:TILES] + right[:TILES]
    total_sibling = send(total, TO_CORE)

    own = standardize(whole, total, part, other)
    own = own, send(own, TO_CORE)
    n1 = other_half(*own, mark(own[0]), total_sibling)
    go_0, stay_0 = products([own], [own], [n1])
    n1 = send(n1, TO_SAME)
    got_0 = send(go_0, TO_Z_FIRST)
    n0, passed = standardize_near(*n0, total, total_sibling, right, left, go_0)
    n0, x2 = (n0,), (send(passed, TO_SAME),)
    go_1, stay_1 = products([own], [n0], [go_0])
    got_1 = send(go_1, TO_Z_FIRST)
    next_0, stay_0 = second(stay_0, got_0, go_1)
    round_0 = stay_0, send(next_0, TO_Z_SECOND)
    y = standardize(y_counts, total, part_y, next_0)
    y = y, send(y, TO_CORE)
    next_1, stay_1 = second(stay_1, got_1, y[0])
    round_1 = stay_1, send(next_1, TO_Z_SECOND)
    go_2, stay_2 = products([y], [own, n0], [next_1])
    got_2 = send(go_2, TO_Z_FIRST)
    go_3, stay_3 = products_y([own, y], n1, [go_2, round_0[1], round_1[1]])
    got_3 = send(go_3, TO_YHI)
    next_2, stay_2 = second(stay_2, got_2, go_3)
    round_2 = stay_2, send(next_2, TO_Z_SECOND)
    go_4, stay_4 = products([own, y], [x2], [next_2])
    got_4 = send(go_4, TO_Z_FIRST)
    sums_a = summed_z([(*round_0, 0), (*round_1, 0)], [(*round_2, 0), (*round_2, 1)], go_4)
    chunks_a = shared(*sums_a)
    go_3, stay_3 = merge_y(stay_3, got_3, chunks_a[1], mark(sums_a[0]))
    got_3 = send(go_3, TO_Z_FIRST)
    next_4, stay_4 = second(stay_4, got_4, go_3)
    round_4 = stay_4, send(next_4, TO_Z_SECOND)
    next_3, stay_3 = second(stay_3, got_3, next_4)
    got_3 = send(next_3, TO_Z_SECOND)
    sums_c = summed_z([(*round_4, 0)], [(*round_4, 1)], next_3)
    chunks_c = shared(*sums_c)
    keep_b, to_c = share(stay_3, got_3, chunks_c[1], mark(sums_c[0]))
    done_a = presum(*chunks_a, keep_b)
    out = finish(done_a, (keep_b, send(to_c, TO_CORE)), chunks_c, done_a[0])
    return out.reshape(128, 8, 4, 128).transpose(0, 2, 1, 3).reshape(1, 128, 1, 4, SPAN)


def solution(mesh):
    placed = (P("cells", "grow", "gcol", None), P("grow", "gcol", None), P("grow", "gcol", None))
    return jax.shard_map(
        per_device,
        mesh=mesh,
        in_specs=placed,
        out_specs=P("grow", "cells", "gcol", None, None),
        check_vma=False,
    )
```

```python
import jax
import jax.numpy as jnp
import numpy as np
from jax import lax
from jax.experimental import pallas as pl
from jax.experimental.pallas import tpu as pltpu
from jax.sharding import PartitionSpec as P

GENES = 8192
CELLS = 18432
AXES = ("cells", "grow", "gcol")
SIZES = (2, 4, 2, 4, 2)
ROWS = 1152
TILES = ROWS // 128
SPAN = 1024
HALF = 512
QUARTER = 256

ALPHA = 2.0**17 / 9.0e6
BETA = 32700.0 / float(np.log1p(2.0**17))
VMEM = 16 * 1024 * 1024
STREAMED = 48 * 1024 * 1024


def moves(target):
    pairs = []
    for i, at in enumerate(np.ndindex(*SIZES)):
        to = tuple(v % s for v, s in zip(target(*at), SIZES))
        pairs.append((i, int(np.ravel_multi_index(to, SIZES))))
    return pairs


TO_CORE = moves(lambda h, z, c, x, b: (h, z, 1 - c, x, b))
TO_YLO = moves(lambda h, z, c, x, b: (h, z, c, x, 1 - b))
TO_YHI = moves(lambda h, z, c, x, b: (1 - h, z, c, x, b))
TO_YHI_CORE = moves(lambda h, z, c, x, b: (1 - h, z, 1 - c, x, b))
TO_X = [moves(lambda h, z, c, x, b, d=d: (h, z, c, x + d, b)) for d in (1, 2, 3)]
FIRST = (1, 3)
TO_Z_FIRST = moves(lambda h, z, c, x, b: (h, z ^ FIRST[c], c, x, b))
TO_Z_SECOND = moves(lambda h, z, c, x, b: (h, z ^ FIRST[1 - c], c, x, b))
TO_SAME = moves(lambda h, z, c, x, b: (h, z, c, x - 1 + 2 * c, b))
TO_CROSS = moves(lambda h, z, c, x, b: (h, z, 1 - c, x + 1 - 2 * c, b))

def here():
    cells = lax.axis_index("cells")
    return cells >> 3, (cells >> 1) & 3, cells & 1, lax.axis_index("grow"), lax.axis_index("gcol")


def z_rows():
    _, z, core, _, _ = here()
    return [(z ^ d) * QUARTER for d in (0, 3 - 2 * core)], [(z ^ d) * QUARTER for d in (1 + 2 * core, 2)]


def out_place(chunk, other):
    _, _, core, x, _ = here()
    core = 1 - core if other else core
    near = (x + 1 - 2 * core) & 3
    block, half = ((x, core), (near, core), (near, 1 - core), (x ^ 2, core))[chunk]
    return half * 16 + block


def send(value, pairs):
    return lax.ppermute(value, AXES, pairs)


def encode(total):
    size = jnp.log(1.0 + ALPHA * jnp.abs(total)) * BETA + 0.5
    code = size.astype(jnp.int32)
    return jnp.where(total < 0, -code, code).astype(jnp.int16)


def decode(code):
    code = code.astype(jnp.int32).astype(jnp.float32)
    size = (jnp.exp(jnp.abs(code) * (1.0 / BETA)) - 1.0) * (1.0 / ALPHA)
    return jnp.where(code < 0, -size, size)


def params(vmem=VMEM, flops=30_000_000_000):
    return dict(
        compiler_params=pltpu.CompilerParams(vmem_limit_bytes=vmem),
        cost_estimate=pl.CostEstimate(flops=flops, bytes_accessed=1_000_000, transcendentals=0),
    )


HELD = pl.BlockSpec(memory_space=pltpu.VMEM)
LOOSE = pl.BlockSpec()
ANYWHERE = pl.BlockSpec(memory_space=pl.ANY)


def of(shape, dtype):
    return jax.ShapeDtypeStruct(shape, dtype)


def take(counts, mean, scale):
    def body(counts_ref, mean_ref, scale_ref, out_ref, narrow_ref, first_ref, other_ref, counts_v, mean_v, scale_v, sems):
        _, _, core, _, _ = here()
        parts = []
        for i in range(TILES):
            rows = pl.ds(i * 1024, 1024)
            parts.append(pltpu.make_async_copy(counts_ref.at[rows], counts_v.at[rows], sems.at[i]))
        genes = [
            pltpu.make_async_copy(mean_ref, mean_v, sems.at[TILES]),
            pltpu.make_async_copy(scale_ref, scale_v, sems.at[TILES + 1]),
        ]
        for c in parts + genes:
            c.start()
        for i in range(TILES):
            parts[i].wait()
            total = None
            at = slice(i * 128, (i + 1) * 128)
            for j in range(8):
                value = counts_v[pl.ds(i * 1024 + j, 128, stride=8), :]
                narrow_ref[at, j * 128 : (j + 1) * 128] = value.astype(jnp.int16)
                total = value if total is None else total + value
            for low, (low_ref, high_ref) in enumerate(((first_ref, other_ref), (other_ref, first_ref))):

                @pl.when(core == low)
                def _():
                    low_ref[at, :] = narrow_ref[at, 0:HALF]
                    high_ref[at, :] = narrow_ref[at, HALF:SPAN]

            out_ref[i : i + 1, :] = jnp.sum(total.astype(jnp.float32).T, axis=0, keepdims=True)
        for c in genes:
            c.wait()
        inverse = 1.0 / scale_v[...]
        out_ref[TILES : TILES + 8, :] = inverse
        out_ref[TILES + 8 : TILES + 16, :] = mean_v[...] * inverse

    return pl.pallas_call(
        body,
        out_shape=(of((TILES + 16, 128), jnp.float32), of((ROWS, SPAN), jnp.int16)) + (of((ROWS, HALF), jnp.int16),) * 2,
        in_specs=[pl.BlockSpec(memory_space=pltpu.HBM)] * 3,
        out_specs=(LOOSE, HELD, HELD, HELD),
        scratch_shapes=[
            pltpu.VMEM((ROWS * 8, 128), jnp.int32),
            pltpu.VMEM((8, 128), jnp.float32),
            pltpu.VMEM((8, 128), jnp.float32),
            pltpu.SemaphoreType.DMA((TILES + 2,)),
        ],
        **params(STREAMED),
    )(counts, mean, scale)


def gate(arrays, after):
    n = len(arrays)
    return pl.pallas_call(
        lambda *refs: None,
        out_shape=tuple(of(a.shape, a.dtype) for a in arrays),
        in_specs=[pl.BlockSpec(memory_space=pl.ANY)] * (n + 1),
        out_specs=[pl.BlockSpec(memory_space=pl.ANY)] * n,
        input_output_aliases={k: k for k in range(n)},
        **params(),
    )(*arrays, after)


def join(part, part_y, after):
    def body(part_ref, y_ref, after_ref, out_ref):
        out_ref[0:TILES, :] = part_ref[0:TILES, :] + y_ref[0:TILES, :]
        out_ref[TILES:, :] = part_ref[TILES:, :]

    return pl.pallas_call(
        body,
        out_shape=of(part.shape, part.dtype),
        in_specs=[LOOSE, LOOSE, ANYWHERE],
        out_specs=LOOSE,
        **params(),
    )(part, part_y, after)


def spread(total_refs, factor_v):
    for k in range(TILES):
        row = sum(ref[k : k + 1, :] for ref in total_refs)
        factor_v[k * 128 : (k + 1) * 128, :] = jnp.broadcast_to(GENES / row, (128, 128)).T


def standardized(count, factor, inverse, shift):
    value = count.astype(jnp.int32).astype(jnp.float32)
    return (jnp.log(1.0 + value * factor) * inverse - shift).astype(jnp.bfloat16)


def by_tiles(run):
    def step(t, carry):
        run(pl.multiple_of(t * 128, 128))
        return carry

    lax.fori_loop(0, TILES, step, 0)


def standardize(counts, total, gene, after):
    def body(counts_ref, total_ref, gene_ref, after_ref, out_ref, factor_v):
        spread([total_ref], factor_v)

        def tile(at):
            rows = pl.ds(at, 128)
            factor = factor_v[rows, :]
            for j in range(8):
                lanes = slice(j * 128, (j + 1) * 128)
                inverse, shift = gene_ref[TILES + j : TILES + j + 1, :], gene_ref[TILES + 8 + j : TILES + 9 + j, :]
                out_ref[rows, lanes] = standardized(counts_ref[rows, lanes], factor, inverse, shift)

        by_tiles(tile)

    return pl.pallas_call(
        body,
        out_shape=of((ROWS, SPAN), jnp.bfloat16),
        in_specs=[HELD, HELD, HELD, ANYWHERE],
        out_specs=HELD,
        scratch_shapes=[pltpu.VMEM((ROWS, 128), jnp.float32)],
        **params(),
    )(counts, total, gene, after)


def mark(after):
    def body(after_ref, out_ref):
        out_ref[...] = jnp.zeros((8, 128), jnp.float32)

    return pl.pallas_call(
        body, out_shape=of((8, 128), jnp.float32), in_specs=[ANYWHERE], out_specs=HELD, **params()
    )(after)


def other_half(mine, sibling, *after):
    def body(mine_ref, sibling_ref, *rest):
        out_ref = rest[-1]
        _, _, core, _, _ = here()

        def run(lanes):
            def tile(at):
                out_ref[pl.ds(at, 128), :] = mine_ref[pl.ds(at, 128), lanes]
                out_ref[pl.ds(at + ROWS, 128), :] = sibling_ref[pl.ds(at, 128), lanes]

            by_tiles(tile)

        @pl.when(core == 0)
        def _():
            run(slice(HALF, SPAN))

        @pl.when(core != 0)
        def _():
            run(slice(0, HALF))

    return pl.pallas_call(
        body,
        out_shape=of((2 * ROWS, HALF), mine.dtype),
        in_specs=[HELD, HELD] + [ANYWHERE] * len(after),
        out_specs=HELD,
        **params(),
    )(mine, sibling, *after)


def standardize_near(mine, sibling, total, total_sibling, right, left, after):
    def body(mine_ref, sibling_ref, t_ref, ts_ref, right_ref, left_ref, after_ref, out_ref, copy_ref, factor_v, gene_v):
        _, _, core, _, _ = here()
        gene_v[...] = jnp.where(core == 0, right_ref[...], left_ref[...])
        for part, count_ref, total_ref in ((0, mine_ref, t_ref), (1, sibling_ref, ts_ref)):
            spread([total_ref], factor_v)

            def tile(at, part=part, count_ref=count_ref):
                factor = factor_v[pl.ds(at, 128), :]
                for j in range(4):
                    lanes = slice(j * 128, (j + 1) * 128)
                    g = TILES + core * 4 + j
                    inverse, shift = gene_v[pl.ds(g, 1), :], gene_v[pl.ds(g + 8, 1), :]
                    value = standardized(count_ref[pl.ds(at, 128), lanes], factor, inverse, shift)
                    out_ref[pl.ds(at + part * ROWS, 128), lanes] = value
                    copy_ref[pl.ds(at + part * ROWS, 128), lanes] = value

            by_tiles(tile)

    return pl.pallas_call(
        body,
        out_shape=(of((2 * ROWS, HALF), jnp.bfloat16),) * 2,
        in_specs=[HELD] * 6 + [ANYWHERE],
        out_specs=(HELD, HELD),
        scratch_shapes=[pltpu.VMEM((ROWS, 128), jnp.float32), pltpu.VMEM((TILES + 16, 128), jnp.float32)],
        **params(),
    )(mine, sibling, total, total_sibling, right, left, after)


def products(rows, cols, after, far=False):
    n_rows, n_cols = len(rows), len(cols)
    units = max(n_rows, n_cols)
    flat = [a for block in rows + cols for a in block]

    def body(*refs):
        go_ref, stay_ref, *scratch = refs[len(flat) + len(after) :]
        _, _, core, _, _ = here()
        stays, goes = z_rows()
        blocks, k = [], 0
        for block in rows + cols:
            blocks.append(refs[k : k + len(block)])
            k += len(block)

        copies = []
        if far:
            col_v, sems = scratch
            for part in range(2):
                half = pl.ds(part * ROWS, ROWS)
                copies.append(pltpu.make_async_copy(blocks[-1][0].at[half], col_v.at[half], sems.at[part]))
                copies[part].start()
            blocks[-1] = (col_v,)

        def right(col, part):
            if len(col) == 1:
                return col[0][part * ROWS : (part + 1) * ROWS, :]
            if col[part].shape[1] == SPAN:
                return col[part][:, pl.ds(pl.multiple_of(core * HALF, HALF), HALF)]
            return col[part][...]

        for unit in range(units):
            row = blocks[unit if n_rows > 1 else 0]
            col = blocks[n_rows + (unit if n_cols > 1 else 0)]

            def product(at):
                at = pl.multiple_of(at, QUARTER)
                terms = []
                for part in range(2):
                    if copies:
                        copies.pop(0).wait()
                    terms.append(
                        lax.dot_general(
                            row[part][:, pl.ds(at, QUARTER)],
                            right(col, part),
                            (((0,), (0,)), ((), ())),
                            preferred_element_type=jnp.float32,
                        )
                    )
                return terms[0] + terms[1]

            for k in range(2):
                go_ref[unit, k] = encode(product(goes[k]))
            for k in range(2):
                stay_ref[unit, k] = product(stays[k])

    return pl.pallas_call(
        body,
        out_shape=(of((units, 2, QUARTER, HALF), jnp.int16), of((units, 2, QUARTER, HALF), jnp.float32)),
        in_specs=[HELD] * (len(flat) - far) + [pl.BlockSpec(memory_space=pltpu.HBM)] * far + [ANYWHERE] * len(after),
        out_specs=(HELD, HELD),
        scratch_shapes=[pltpu.VMEM((2 * ROWS, HALF), jnp.bfloat16), pltpu.SemaphoreType.DMA((2,))] if far else [],
        **params(flops=12_000_000_000),
    )(*flat, *after)


def products_y(rows, col, after):
    flat = [a for block in rows for a in block]

    def body(*refs):
        col_ref = refs[len(flat)]
        go_ref, stay_ref, col_v, sems = refs[len(flat) + 1 + len(after) :]
        copies = []
        for part in range(2):
            half = pl.ds(part * ROWS, ROWS)
            copies.append(pltpu.make_async_copy(col_ref.at[half], col_v.at[half], sems.at[part]))
            copies[part].start()
        high, _, _, _, low = here()
        away = high ^ low
        def run(units):
            waits = list(copies)
            for unit, goes in units:
                mine, sibling = refs[2 * unit : 2 * unit + 2]
                for z in range(4):
                    lanes = slice(z * QUARTER, (z + 1) * QUARTER)
                    terms = []
                    for part, block in ((0, mine), (1, sibling)):
                        if waits:
                            waits.pop(0).wait()
                        terms.append(
                            lax.dot_general(
                                block[:, lanes],
                                col_v[part * ROWS : (part + 1) * ROWS, :],
                                (((0,), (0,)), ((), ())),
                                preferred_element_type=jnp.float32,
                            )
                        )
                    if goes:
                        go_ref[z] = encode(terms[0] + terms[1])
                    else:
                        stay_ref[z] = terms[0] + terms[1]

        @pl.when(away == 0)
        def _():
            run(((1, True), (0, False)))

        @pl.when(away != 0)
        def _():
            run(((0, True), (1, False)))

    return pl.pallas_call(
        body,
        out_shape=(of((4, QUARTER, HALF), jnp.int16), of((4, QUARTER, HALF), jnp.float32)),
        in_specs=[HELD] * len(flat) + [pl.BlockSpec(memory_space=pltpu.HBM)] + [ANYWHERE] * len(after),
        out_specs=(HELD, HELD),
        scratch_shapes=[pltpu.VMEM((2 * ROWS, HALF), jnp.bfloat16), pltpu.SemaphoreType.DMA((2,))],
        **params(flops=12_000_000_000),
    )(*flat, col, *after)


def merge_y(stay, got, *after):
    def body(stay_ref, got_ref, *rest):
        go_ref, out_ref = rest[-2:]
        _, z, core, _, _ = here()
        for k, d in enumerate((1 + 2 * core, 2)):
            go_ref[0, k] = encode(stay_ref[z ^ d] + decode(got_ref[z ^ d]))
        for k, d in enumerate((0, 3 - 2 * core)):
            out_ref[0, k] = stay_ref[z ^ d] + decode(got_ref[z ^ d])

    return pl.pallas_call(
        body,
        out_shape=(of((1, 2, QUARTER, HALF), jnp.int16), of((1, 2, QUARTER, HALF), jnp.float32)),
        in_specs=[LOOSE, LOOSE] + [ANYWHERE] * len(after),
        out_specs=(LOOSE, LOOSE),
        **params(),
    )(stay, got, *after)


def share(stay, got, *after):
    def body(stay_ref, got_ref, *rest):
        keep, to_c, total = rest[-3:]
        _, _, core, _, _ = here()
        total[...] = stay_ref[0] + decode(got_ref[0])
        keep[0] = total[pl.ds(pl.multiple_of(core * 128, 128), 128), :]
        to_c[0] = encode(total[pl.ds(pl.multiple_of((1 - core) * 128, 128), 128), :])

    return pl.pallas_call(
        body,
        out_shape=(of((1, 128, HALF), jnp.float32), of((1, 128, HALF), jnp.int16)),
        in_specs=[LOOSE, LOOSE] + [ANYWHERE] * len(after),
        out_specs=(LOOSE, LOOSE),
        scratch_shapes=[pltpu.VMEM((QUARTER, HALF), jnp.float32)],
        **params(),
    )(stay, got, *after)


def second(stay, got, after):
    units = stay.shape[0]

    def body(stay_ref, got_ref, after_ref, go_ref, out_ref):
        for u in range(units):
            go_ref[u] = encode(stay_ref[u, 1] + decode(got_ref[u, 1]))
            out_ref[u] = stay_ref[u, 0] + decode(got_ref[u, 0])

    return pl.pallas_call(
        body,
        out_shape=(of((units, QUARTER, HALF), jnp.int16), of((units, QUARTER, HALF), jnp.float32)),
        in_specs=[LOOSE, LOOSE, ANYWHERE],
        out_specs=(LOOSE, LOOSE),
        **params(),
    )(stay, got, after)


def summed_z(own, other, after):
    chunks = len(own)
    arrays = []
    for stay, got, _ in own + other:
        if not any(stay is a for a in arrays):
            arrays += [stay, got]
    places = [next(i for i, a in enumerate(arrays) if a is stay) for stay, _, _ in own + other]

    def body(*refs):
        keep, to_c, to_y, to_yc, total = refs[len(arrays) + 1 :]
        high, _, core, _, low = here()
        away = high ^ low
        mine = pl.ds(pl.multiple_of(core * 128, 128), 128)
        others = pl.ds(pl.multiple_of((1 - core) * 128, 128), 128)
        for k in range(chunks):
            for side in range(2):
                n = side * chunks + k
                unit = (own + other)[n][2]
                total[k, side] = refs[places[n]][unit] + decode(refs[places[n] + 1][unit])
            to_y[k] = encode(total[k, 1 - away, mine, :])
            to_yc[k] = encode(total[k, 1 - away, others, :])
            to_c[k] = encode(total[k, away, others, :])
            keep[k] = total[k, away, mine, :]

    return pl.pallas_call(
        body,
        out_shape=(of((chunks, 128, HALF), jnp.float32),) + (of((chunks, 128, HALF), jnp.int16),) * 3,
        in_specs=[LOOSE] * len(arrays) + [ANYWHERE],
        out_specs=(LOOSE,) * 4,
        scratch_shapes=[pltpu.VMEM((chunks, 2, QUARTER, HALF), jnp.float32)],
        **params(),
    )(*arrays, after)


def presum(keep, got_c, got_y, got_yc, after):
    def body(keep_ref, c_ref, y_ref, yc_ref, after_ref, mine_ref, others_ref):
        for k in range(keep.shape[0]):
            mine_ref[k] = keep_ref[k] + decode(y_ref[k])
            others_ref[k] = decode(c_ref[k]) + decode(yc_ref[k])

    return pl.pallas_call(
        body,
        out_shape=(of(keep.shape, jnp.float32),) * 2,
        in_specs=[LOOSE] * 4 + [ANYWHERE],
        out_specs=(LOOSE, LOOSE),
        **params(),
    )(keep, got_c, got_y, got_yc, after)


def finish(done, chunk_2, chunk_3, after):
    rows = 32

    def body(mine_ref, others_ref, keep_2, c_2, keep_3, c_3, y_3, yc_3, after_ref, out_ref):
        def put(chunk, mine, others):
            for other, value in ((False, mine), (True, others)):
                value = value * (1.0 / CELLS)
                base = out_place(chunk, other)
                for q in range(4):
                    out_ref[pl.ds(base + 4 * q, rows, stride=32), :] = value[:, q * 128 : (q + 1) * 128]

        for k in range(2):
            put(k, mine_ref[k], others_ref[k])
        put(2, keep_2[0], decode(c_2[0]))
        put(3, keep_3[0] + decode(y_3[0]), decode(c_3[0]) + decode(yc_3[0]))

    def block(n):
        return pl.BlockSpec((n, rows, HALF), lambda i: (0, i, 0))

    return pl.pallas_call(
        body,
        out_shape=of((4096, 128), jnp.float32),
        grid=(128 // rows,),
        in_specs=[block(2)] * 2 + [block(1)] * 6 + [ANYWHERE],
        out_specs=pl.BlockSpec((rows * 32, 128), lambda i: (i, 0)),
        **params(),
    )(*done, *chunk_2, *chunk_3, after)


def shared(stay, to_c, to_y, to_yc):
    return stay, send(to_c, TO_CORE), send(to_y, TO_YHI), send(to_yc, TO_YHI_CORE)


def per_device(counts, gene_mean, gene_scale):
    counts = counts.reshape(ROWS * 8, 128)

    part, whole, first, other = take(counts, gene_mean.reshape(8, 128), gene_scale.reshape(8, 128))
    part_y = send(part, TO_YLO)
    (whole,) = gate([whole], part)
    y_counts = send(whole, TO_YLO)
    pair = join(part, part_y, whole)
    left, opposite, right = [send(pair, to) for to in TO_X]
    first, other = gate([first, other], pair)
    n0 = send(first, TO_SAME), send(other, TO_CROSS)
    total = pair[:TILES] + left[:TILES] + opposite[:TILES] + right[:TILES]
    total_sibling = send(total, TO_CORE)

    own = standardize(whole, total, part, other)
    own = own, send(own, TO_CORE)
    n1 = other_half(*own, mark(own[0]), total_sibling)
    go_0, stay_0 = products([own], [own], [n1])
    n1 = send(n1, TO_SAME)
    got_0 = send(go_0, TO_Z_FIRST)
    n0, passed = standardize_near(*n0, total, total_sibling, right, left, go_0)
    n0, x2 = (n0,), (send(passed, TO_SAME),)
    go_1, stay_1 = products([own], [n0], [go_0])
    got_1 = send(go_1, TO_Z_FIRST)
    next_0, stay_0 = second(stay_0, got_0, go_1)
    round_0 = stay_0, send(next_0, TO_Z_SECOND)
    y = standardize(y_counts, total, part_y, next_0)
    y = y, send(y, TO_CORE)
    next_1, stay_1 = second(stay_1, got_1, y[0])
    round_1 = stay_1, send(next_1, TO_Z_SECOND)
    go_2, stay_2 = products([y], [own, n0], [next_1])
    got_2 = send(go_2, TO_Z_FIRST)
    go_3, stay_3 = products_y([own, y], n1, [go_2, round_0[1], round_1[1]])
    got_3 = send(go_3, TO_YHI)
    next_2, stay_2 = second(stay_2, got_2, go_3)
    round_2 = stay_2, send(next_2, TO_Z_SECOND)
    go_4, stay_4 = products([own, y], [x2], [next_2])
    got_4 = send(go_4, TO_Z_FIRST)
    sums_a = summed_z([(*round_0, 0), (*round_1, 0)], [(*round_2, 0), (*round_2, 1)], go_4)
    chunks_a = shared(*sums_a)
    go_3, stay_3 = merge_y(stay_3, got_3, chunks_a[1], mark(sums_a[0]))
    got_3 = send(go_3, TO_Z_FIRST)
    next_4, stay_4 = second(stay_4, got_4, go_3)
    round_4 = stay_4, send(next_4, TO_Z_SECOND)
    next_3, stay_3 = second(stay_3, got_3, next_4)
    got_3 = send(next_3, TO_Z_SECOND)
    sums_c = summed_z([(*round_4, 0)], [(*round_4, 1)], next_3)
    chunks_c = shared(*sums_c)
    keep_b, to_c = share(stay_3, got_3, chunks_c[1], mark(sums_c[0]))
    done_a = presum(*chunks_a, keep_b)
    out = finish(done_a, (keep_b, send(to_c, TO_CORE)), chunks_c, done_a[0])
    return out.reshape(128, 8, 4, 128).transpose(0, 2, 1, 3).reshape(1, 128, 1, 4, SPAN)


def solution(mesh):
    placed = (P("cells", "grow", "gcol", None), P("grow", "gcol", None), P("grow", "gcol", None))
    return jax.shard_map(
        per_device,
        mesh=mesh,
        in_specs=placed,
        out_specs=P("grow", "cells", "gcol", None, None),
        check_vma=False,
    )
```

```python
import jax
import jax.numpy as jnp
import numpy as np
from jax import lax
from jax.experimental import pallas as pl
from jax.experimental.pallas import tpu as pltpu
from jax.sharding import PartitionSpec as P

GENES = 8192
CELLS = 18432
AXES = ("cells", "grow", "gcol")
SIZES = (2, 4, 2, 4, 2)
ROWS = 1152
TILES = ROWS // 128
SPAN = 1024
HALF = 512
QUARTER = 256

ALPHA = 2.0**17 / 9.0e6
BETA = 32700.0 / float(np.log1p(2.0**17))
VMEM = 16 * 1024 * 1024
STREAMED = 48 * 1024 * 1024


def moves(target):
    pairs = []
    for i, at in enumerate(np.ndindex(*SIZES)):
        to = tuple(v % s for v, s in zip(target(*at), SIZES))
        pairs.append((i, int(np.ravel_multi_index(to, SIZES))))
    return pairs


TO_CORE = moves(lambda h, z, c, x, b: (h, z, 1 - c, x, b))
TO_YLO = moves(lambda h, z, c, x, b: (h, z, c, x, 1 - b))
TO_YHI = moves(lambda h, z, c, x, b: (1 - h, z, c, x, b))
TO_YHI_CORE = moves(lambda h, z, c, x, b: (1 - h, z, 1 - c, x, b))
TO_X = [moves(lambda h, z, c, x, b, d=d: (h, z, c, x + d, b)) for d in (1, 2, 3)]
FIRST = (1, 3)
TO_Z_FIRST = moves(lambda h, z, c, x, b: (h, z ^ FIRST[c], c, x, b))
TO_Z_SECOND = moves(lambda h, z, c, x, b: (h, z ^ FIRST[1 - c], c, x, b))
TO_SAME = moves(lambda h, z, c, x, b: (h, z, c, x - 1 + 2 * c, b))
TO_CROSS = moves(lambda h, z, c, x, b: (h, z, 1 - c, x + 1 - 2 * c, b))

def here():
    cells = lax.axis_index("cells")
    return cells >> 3, (cells >> 1) & 3, cells & 1, lax.axis_index("grow"), lax.axis_index("gcol")


def z_rows():
    _, z, core, _, _ = here()
    return [(z ^ d) * QUARTER for d in (0, 3 - 2 * core)], [(z ^ d) * QUARTER for d in (1 + 2 * core, 2)]


def out_place(chunk, other):
    _, _, core, x, _ = here()
    core = 1 - core if other else core
    near = (x + 1 - 2 * core) & 3
    block, half = ((x, core), (near, core), (near, 1 - core), (x ^ 2, core))[chunk]
    return half * 16 + block


def send(value, pairs):
    return lax.ppermute(value, AXES, pairs)


def encode(total):
    size = jnp.log(1.0 + ALPHA * jnp.abs(total)) * BETA + 0.5
    code = size.astype(jnp.int32)
    return jnp.where(total < 0, -code, code).astype(jnp.int16)


def decode(code):
    code = code.astype(jnp.int32).astype(jnp.float32)
    size = (jnp.exp(jnp.abs(code) * (1.0 / BETA)) - 1.0) * (1.0 / ALPHA)
    return jnp.where(code < 0, -size, size)


def params(vmem=VMEM, flops=30_000_000_000):
    return dict(
        compiler_params=pltpu.CompilerParams(vmem_limit_bytes=vmem),
        cost_estimate=pl.CostEstimate(flops=flops, bytes_accessed=1_000_000, transcendentals=0),
    )


HELD = pl.BlockSpec(memory_space=pltpu.VMEM)
LOOSE = pl.BlockSpec()
ANYWHERE = pl.BlockSpec(memory_space=pl.ANY)


def of(shape, dtype):
    return jax.ShapeDtypeStruct(shape, dtype)


def take(counts, mean, scale):
    def body(counts_ref, mean_ref, scale_ref, out_ref, narrow_ref, first_ref, other_ref, counts_v, mean_v, scale_v, sems):
        _, _, core, _, _ = here()
        parts = []
        for i in range(TILES):
            rows = pl.ds(i * 1024, 1024)
            parts.append(pltpu.make_async_copy(counts_ref.at[rows], counts_v.at[rows], sems.at[i]))
        genes = [
            pltpu.make_async_copy(mean_ref, mean_v, sems.at[TILES]),
            pltpu.make_async_copy(scale_ref, scale_v, sems.at[TILES + 1]),
        ]
        for c in parts + genes:
            c.start()
        for i in range(TILES):
            parts[i].wait()
            total = None
            at = slice(i * 128, (i + 1) * 128)
            for j in range(8):
                value = counts_v[pl.ds(i * 1024 + j, 128, stride=8), :]
                narrow_ref[at, j * 128 : (j + 1) * 128] = value.astype(jnp.int16)
                total = value if total is None else total + value
            for low, (low_ref, high_ref) in enumerate(((first_ref, other_ref), (other_ref, first_ref))):

                @pl.when(core == low)
                def _():
                    low_ref[at, :] = narrow_ref[at, 0:HALF]
                    high_ref[at, :] = narrow_ref[at, HALF:SPAN]

            out_ref[i : i + 1, :] = jnp.sum(total.astype(jnp.float32).T, axis=0, keepdims=True)
        for c in genes:
            c.wait()
        inverse = 1.0 / scale_v[...]
        out_ref[TILES : TILES + 8, :] = inverse
        out_ref[TILES + 8 : TILES + 16, :] = mean_v[...] * inverse

    return pl.pallas_call(
        body,
        out_shape=(of((TILES + 16, 128), jnp.float32), of((ROWS, SPAN), jnp.int16)) + (of((ROWS, HALF), jnp.int16),) * 2,
        in_specs=[pl.BlockSpec(memory_space=pltpu.HBM)] * 3,
        out_specs=(LOOSE, HELD, HELD, HELD),
        scratch_shapes=[
            pltpu.VMEM((ROWS * 8, 128), jnp.int32),
            pltpu.VMEM((8, 128), jnp.float32),
            pltpu.VMEM((8, 128), jnp.float32),
            pltpu.SemaphoreType.DMA((TILES + 2,)),
        ],
        **params(STREAMED),
    )(counts, mean, scale)


def gate(arrays, after):
    n = len(arrays)
    return pl.pallas_call(
        lambda *refs: None,
        out_shape=tuple(of(a.shape, a.dtype) for a in arrays),
        in_specs=[pl.BlockSpec(memory_space=pl.ANY)] * (n + 1),
        out_specs=[pl.BlockSpec(memory_space=pl.ANY)] * n,
        input_output_aliases={k: k for k in range(n)},
        **params(),
    )(*arrays, after)


def join(part, part_y, after):
    def body(part_ref, y_ref, after_ref, out_ref):
        out_ref[0:TILES, :] = part_ref[0:TILES, :] + y_ref[0:TILES, :]
        out_ref[TILES:, :] = part_ref[TILES:, :]

    return pl.pallas_call(
        body,
        out_shape=of(part.shape, part.dtype),
        in_specs=[LOOSE, LOOSE, ANYWHERE],
        out_specs=LOOSE,
        **params(),
    )(part, part_y, after)


def spread(total_refs, factor_v):
    for k in range(TILES):
        row = sum(ref[k : k + 1, :] for ref in total_refs)
        factor_v[k * 128 : (k + 1) * 128, :] = jnp.broadcast_to(GENES / row, (128, 128)).T


def standardized(count, factor, inverse, shift):
    value = count.astype(jnp.int32).astype(jnp.float32)
    return (jnp.log(1.0 + value * factor) * inverse - shift).astype(jnp.bfloat16)


def by_tiles(run):
    def step(t, carry):
        run(pl.multiple_of(t * 128, 128))
        return carry

    lax.fori_loop(0, TILES, step, 0, unroll=3)


def standardize(counts, total, gene, after):
    def body(counts_ref, total_ref, gene_ref, after_ref, out_ref, factor_v):
        spread([total_ref], factor_v)

        def tile(at):
            rows = pl.ds(at, 128)
            factor = factor_v[rows, :]
            for j in range(8):
                lanes = slice(j * 128, (j + 1) * 128)
                inverse, shift = gene_ref[TILES + j : TILES + j + 1, :], gene_ref[TILES + 8 + j : TILES + 9 + j, :]
                out_ref[rows, lanes] = standardized(counts_ref[rows, lanes], factor, inverse, shift)

        by_tiles(tile)

    return pl.pallas_call(
        body,
        out_shape=of((ROWS, SPAN), jnp.bfloat16),
        in_specs=[HELD, HELD, HELD, ANYWHERE],
        out_specs=HELD,
        scratch_shapes=[pltpu.VMEM((ROWS, 128), jnp.float32)],
        **params(),
    )(counts, total, gene, after)


def mark(after):
    def body(after_ref, out_ref):
        out_ref[...] = jnp.zeros((8, 128), jnp.float32)

    return pl.pallas_call(
        body, out_shape=of((8, 128), jnp.float32), in_specs=[ANYWHERE], out_specs=HELD, **params()
    )(after)


def other_half(mine, sibling, *after):
    def body(mine_ref, sibling_ref, *rest):
        out_ref = rest[-1]
        _, _, core, _, _ = here()

        def run(lanes):
            def tile(at):
                out_ref[pl.ds(at, 128), :] = mine_ref[pl.ds(at, 128), lanes]
                out_ref[pl.ds(at + ROWS, 128), :] = sibling_ref[pl.ds(at, 128), lanes]

            by_tiles(tile)

        @pl.when(core == 0)
        def _():
            run(slice(HALF, SPAN))

        @pl.when(core != 0)
        def _():
            run(slice(0, HALF))

    return pl.pallas_call(
        body,
        out_shape=of((2 * ROWS, HALF), mine.dtype),
        in_specs=[HELD, HELD] + [ANYWHERE] * len(after),
        out_specs=HELD,
        **params(),
    )(mine, sibling, *after)


def standardize_near(mine, sibling, total, total_sibling, right, left, after):
    def body(mine_ref, sibling_ref, t_ref, ts_ref, right_ref, left_ref, after_ref, out_ref, copy_ref, factor_v, gene_v):
        _, _, core, _, _ = here()
        gene_v[...] = jnp.where(core == 0, right_ref[...], left_ref[...])
        for part, count_ref, total_ref in ((0, mine_ref, t_ref), (1, sibling_ref, ts_ref)):
            spread([total_ref], factor_v)

            def tile(at, part=part, count_ref=count_ref):
                factor = factor_v[pl.ds(at, 128), :]
                for j in range(4):
                    lanes = slice(j * 128, (j + 1) * 128)
                    g = TILES + core * 4 + j
                    inverse, shift = gene_v[pl.ds(g, 1), :], gene_v[pl.ds(g + 8, 1), :]
                    value = standardized(count_ref[pl.ds(at, 128), lanes], factor, inverse, shift)
                    out_ref[pl.ds(at + part * ROWS, 128), lanes] = value
                    copy_ref[pl.ds(at + part * ROWS, 128), lanes] = value

            by_tiles(tile)

    return pl.pallas_call(
        body,
        out_shape=(of((2 * ROWS, HALF), jnp.bfloat16),) * 2,
        in_specs=[HELD] * 6 + [ANYWHERE],
        out_specs=(HELD, HELD),
        scratch_shapes=[pltpu.VMEM((ROWS, 128), jnp.float32), pltpu.VMEM((TILES + 16, 128), jnp.float32)],
        **params(),
    )(mine, sibling, total, total_sibling, right, left, after)


def products(rows, cols, after, far=False):
    n_rows, n_cols = len(rows), len(cols)
    units = max(n_rows, n_cols)
    flat = [a for block in rows + cols for a in block]

    def body(*refs):
        go_ref, stay_ref, *scratch = refs[len(flat) + len(after) :]
        _, _, core, _, _ = here()
        stays, goes = z_rows()
        blocks, k = [], 0
        for block in rows + cols:
            blocks.append(refs[k : k + len(block)])
            k += len(block)

        copies = []
        if far:
            col_v, sems = scratch
            for part in range(2):
                half = pl.ds(part * ROWS, ROWS)
                copies.append(pltpu.make_async_copy(blocks[-1][0].at[half], col_v.at[half], sems.at[part]))
                copies[part].start()
            blocks[-1] = (col_v,)

        def right(col, part):
            if len(col) == 1:
                return col[0][part * ROWS : (part + 1) * ROWS, :]
            if col[part].shape[1] == SPAN:
                return col[part][:, pl.ds(pl.multiple_of(core * HALF, HALF), HALF)]
            return col[part][...]

        for unit in range(units):
            row = blocks[unit if n_rows > 1 else 0]
            col = blocks[n_rows + (unit if n_cols > 1 else 0)]

            def product(at):
                at = pl.multiple_of(at, QUARTER)
                terms = []
                for part in range(2):
                    if copies:
                        copies.pop(0).wait()
                    terms.append(
                        lax.dot_general(
                            row[part][:, pl.ds(at, QUARTER)],
                            right(col, part),
                            (((0,), (0,)), ((), ())),
                            preferred_element_type=jnp.float32,
                        )
                    )
                return terms[0] + terms[1]

            for k in range(2):
                go_ref[unit, k] = encode(product(goes[k]))
            for k in range(2):
                stay_ref[unit, k] = product(stays[k])

    return pl.pallas_call(
        body,
        out_shape=(of((units, 2, QUARTER, HALF), jnp.int16), of((units, 2, QUARTER, HALF), jnp.float32)),
        in_specs=[HELD] * (len(flat) - far) + [pl.BlockSpec(memory_space=pltpu.HBM)] * far + [ANYWHERE] * len(after),
        out_specs=(HELD, HELD),
        scratch_shapes=[pltpu.VMEM((2 * ROWS, HALF), jnp.bfloat16), pltpu.SemaphoreType.DMA((2,))] if far else [],
        **params(flops=12_000_000_000),
    )(*flat, *after)


def products_y(rows, col, after):
    flat = [a for block in rows for a in block]

    def body(*refs):
        col_ref = refs[len(flat)]
        go_ref, stay_ref, col_v, sems = refs[len(flat) + 1 + len(after) :]
        copies = []
        for part in range(2):
            half = pl.ds(part * ROWS, ROWS)
            copies.append(pltpu.make_async_copy(col_ref.at[half], col_v.at[half], sems.at[part]))
            copies[part].start()
        high, _, _, _, low = here()
        away = high ^ low
        def run(units):
            waits = list(copies)
            for unit, goes in units:
                mine, sibling = refs[2 * unit : 2 * unit + 2]
                for z in range(4):
                    lanes = slice(z * QUARTER, (z + 1) * QUARTER)
                    terms = []
                    for part, block in ((0, mine), (1, sibling)):
                        if waits:
                            waits.pop(0).wait()
                        terms.append(
                            lax.dot_general(
                                block[:, lanes],
                                col_v[part * ROWS : (part + 1) * ROWS, :],
                                (((0,), (0,)), ((), ())),
                                preferred_element_type=jnp.float32,
                            )
                        )
                    if goes:
                        go_ref[z] = encode(terms[0] + terms[1])
                    else:
                        stay_ref[z] = terms[0] + terms[1]

        @pl.when(away == 0)
        def _():
            run(((1, True), (0, False)))

        @pl.when(away != 0)
        def _():
            run(((0, True), (1, False)))

    return pl.pallas_call(
        body,
        out_shape=(of((4, QUARTER, HALF), jnp.int16), of((4, QUARTER, HALF), jnp.float32)),
        in_specs=[HELD] * len(flat) + [pl.BlockSpec(memory_space=pltpu.HBM)] + [ANYWHERE] * len(after),
        out_specs=(HELD, HELD),
        scratch_shapes=[pltpu.VMEM((2 * ROWS, HALF), jnp.bfloat16), pltpu.SemaphoreType.DMA((2,))],
        **params(flops=12_000_000_000),
    )(*flat, col, *after)


def merge_y(stay, got, *after):
    def body(stay_ref, got_ref, *rest):
        go_ref, out_ref = rest[-2:]
        _, z, core, _, _ = here()
        for k, d in enumerate((1 + 2 * core, 2)):
            go_ref[0, k] = encode(stay_ref[z ^ d] + decode(got_ref[z ^ d]))
        for k, d in enumerate((0, 3 - 2 * core)):
            out_ref[0, k] = stay_ref[z ^ d] + decode(got_ref[z ^ d])

    return pl.pallas_call(
        body,
        out_shape=(of((1, 2, QUARTER, HALF), jnp.int16), of((1, 2, QUARTER, HALF), jnp.float32)),
        in_specs=[LOOSE, LOOSE] + [ANYWHERE] * len(after),
        out_specs=(LOOSE, LOOSE),
        **params(),
    )(stay, got, *after)


def share(stay, got, *after):
    def body(stay_ref, got_ref, *rest):
        keep, to_c, total = rest[-3:]
        _, _, core, _, _ = here()
        total[...] = stay_ref[0] + decode(got_ref[0])
        keep[0] = total[pl.ds(pl.multiple_of(core * 128, 128), 128), :]
        to_c[0] = encode(total[pl.ds(pl.multiple_of((1 - core) * 128, 128), 128), :])

    return pl.pallas_call(
        body,
        out_shape=(of((1, 128, HALF), jnp.float32), of((1, 128, HALF), jnp.int16)),
        in_specs=[LOOSE, LOOSE] + [ANYWHERE] * len(after),
        out_specs=(LOOSE, LOOSE),
        scratch_shapes=[pltpu.VMEM((QUARTER, HALF), jnp.float32)],
        **params(),
    )(stay, got, *after)


def second(stay, got, after):
    units = stay.shape[0]

    def body(stay_ref, got_ref, after_ref, go_ref, out_ref):
        for u in range(units):
            go_ref[u] = encode(stay_ref[u, 1] + decode(got_ref[u, 1]))
            out_ref[u] = stay_ref[u, 0] + decode(got_ref[u, 0])

    return pl.pallas_call(
        body,
        out_shape=(of((units, QUARTER, HALF), jnp.int16), of((units, QUARTER, HALF), jnp.float32)),
        in_specs=[LOOSE, LOOSE, ANYWHERE],
        out_specs=(LOOSE, LOOSE),
        **params(),
    )(stay, got, after)


def summed_z(own, other, after):
    chunks = len(own)
    arrays = []
    for stay, got, _ in own + other:
        if not any(stay is a for a in arrays):
            arrays += [stay, got]
    places = [next(i for i, a in enumerate(arrays) if a is stay) for stay, _, _ in own + other]

    def body(*refs):
        keep, to_c, to_y, to_yc, total = refs[len(arrays) + 1 :]
        high, _, core, _, low = here()
        away = high ^ low
        mine = pl.ds(pl.multiple_of(core * 128, 128), 128)
        others = pl.ds(pl.multiple_of((1 - core) * 128, 128), 128)
        for k in range(chunks):
            for side in range(2):
                n = side * chunks + k
                unit = (own + other)[n][2]
                total[k, side] = refs[places[n]][unit] + decode(refs[places[n] + 1][unit])
            to_y[k] = encode(total[k, 1 - away, mine, :])
            to_yc[k] = encode(total[k, 1 - away, others, :])
            to_c[k] = encode(total[k, away, others, :])
            keep[k] = total[k, away, mine, :]

    return pl.pallas_call(
        body,
        out_shape=(of((chunks, 128, HALF), jnp.float32),) + (of((chunks, 128, HALF), jnp.int16),) * 3,
        in_specs=[LOOSE] * len(arrays) + [ANYWHERE],
        out_specs=(LOOSE,) * 4,
        scratch_shapes=[pltpu.VMEM((chunks, 2, QUARTER, HALF), jnp.float32)],
        **params(),
    )(*arrays, after)


def presum(keep, got_c, got_y, got_yc, after):
    def body(keep_ref, c_ref, y_ref, yc_ref, after_ref, mine_ref, others_ref):
        for k in range(keep.shape[0]):
            mine_ref[k] = keep_ref[k] + decode(y_ref[k])
            others_ref[k] = decode(c_ref[k]) + decode(yc_ref[k])

    return pl.pallas_call(
        body,
        out_shape=(of(keep.shape, jnp.float32),) * 2,
        in_specs=[LOOSE] * 4 + [ANYWHERE],
        out_specs=(LOOSE, LOOSE),
        **params(),
    )(keep, got_c, got_y, got_yc, after)


def finish(done, chunk_2, chunk_3, after):
    rows = 32

    def body(mine_ref, others_ref, keep_2, c_2, keep_3, c_3, y_3, yc_3, after_ref, out_ref):
        def put(chunk, mine, others):
            for other, value in ((False, mine), (True, others)):
                value = value * (1.0 / CELLS)
                base = out_place(chunk, other)
                for q in range(4):
                    out_ref[pl.ds(base + 4 * q, rows, stride=32), :] = value[:, q * 128 : (q + 1) * 128]

        for k in range(2):
            put(k, mine_ref[k], others_ref[k])
        put(2, keep_2[0], decode(c_2[0]))
        put(3, keep_3[0] + decode(y_3[0]), decode(c_3[0]) + decode(yc_3[0]))

    def block(n):
        return pl.BlockSpec((n, rows, HALF), lambda i: (0, i, 0))

    return pl.pallas_call(
        body,
        out_shape=of((4096, 128), jnp.float32),
        grid=(128 // rows,),
        in_specs=[block(2)] * 2 + [block(1)] * 6 + [ANYWHERE],
        out_specs=pl.BlockSpec((rows * 32, 128), lambda i: (i, 0)),
        **params(),
    )(*done, *chunk_2, *chunk_3, after)


def shared(stay, to_c, to_y, to_yc):
    return stay, send(to_c, TO_CORE), send(to_y, TO_YHI), send(to_yc, TO_YHI_CORE)


def per_device(counts, gene_mean, gene_scale):
    counts = counts.reshape(ROWS * 8, 128)

    part, whole, first, other = take(counts, gene_mean.reshape(8, 128), gene_scale.reshape(8, 128))
    part_y = send(part, TO_YLO)
    (whole,) = gate([whole], part)
    y_counts = send(whole, TO_YLO)
    pair = join(part, part_y, whole)
    left, opposite, right = [send(pair, to) for to in TO_X]
    first, other = gate([first, other], pair)
    n0 = send(first, TO_SAME), send(other, TO_CROSS)
    total = pair[:TILES] + left[:TILES] + opposite[:TILES] + right[:TILES]
    total_sibling = send(total, TO_CORE)

    own = standardize(whole, total, part, other)
    own = own, send(own, TO_CORE)
    n1 = other_half(*own, mark(own[0]), total_sibling)
    go_0, stay_0 = products([own], [own], [n1])
    n1 = send(n1, TO_SAME)
    got_0 = send(go_0, TO_Z_FIRST)
    n0, passed = standardize_near(*n0, total, total_sibling, right, left, go_0)
    n0, x2 = (n0,), (send(passed, TO_SAME),)
    go_1, stay_1 = products([own], [n0], [go_0])
    got_1 = send(go_1, TO_Z_FIRST)
    next_0, stay_0 = second(stay_0, got_0, go_1)
    round_0 = stay_0, send(next_0, TO_Z_SECOND)
    y = standardize(y_counts, total, part_y, next_0)
    y = y, send(y, TO_CORE)
    next_1, stay_1 = second(stay_1, got_1, y[0])
    round_1 = stay_1, send(next_1, TO_Z_SECOND)
    go_2, stay_2 = products([y], [own, n0], [next_1])
    got_2 = send(go_2, TO_Z_FIRST)
    go_3, stay_3 = products_y([own, y], n1, [go_2, round_0[1], round_1[1]])
    got_3 = send(go_3, TO_YHI)
    next_2, stay_2 = second(stay_2, got_2, go_3)
    round_2 = stay_2, send(next_2, TO_Z_SECOND)
    go_4, stay_4 = products([own, y], [x2], [next_2])
    got_4 = send(go_4, TO_Z_FIRST)
    sums_a = summed_z([(*round_0, 0), (*round_1, 0)], [(*round_2, 0), (*round_2, 1)], go_4)
    chunks_a = shared(*sums_a)
    go_3, stay_3 = merge_y(stay_3, got_3, chunks_a[1], mark(sums_a[0]))
    got_3 = send(go_3, TO_Z_FIRST)
    next_4, stay_4 = second(stay_4, got_4, go_3)
    round_4 = stay_4, send(next_4, TO_Z_SECOND)
    next_3, stay_3 = second(stay_3, got_3, next_4)
    got_3 = send(next_3, TO_Z_SECOND)
    sums_c = summed_z([(*round_4, 0)], [(*round_4, 1)], next_3)
    chunks_c = shared(*sums_c)
    keep_b, to_c = share(stay_3, got_3, chunks_c[1], mark(sums_c[0]))
    done_a = presum(*chunks_a, keep_b)
    out = finish(done_a, (keep_b, send(to_c, TO_CORE)), chunks_c, done_a[0])
    return out.reshape(128, 8, 4, 128).transpose(0, 2, 1, 3).reshape(1, 128, 1, 4, SPAN)


def solution(mesh):
    placed = (P("cells", "grow", "gcol", None), P("grow", "gcol", None), P("grow", "gcol", None))
    return jax.shard_map(
        per_device,
        mesh=mesh,
        in_specs=placed,
        out_specs=P("grow", "cells", "gcol", None, None),
        check_vma=False,
    )
```
